512 devices in a mesh: roll: 64 (over y, z_lo, x), learn: 8 (over z_hi, core).
Axes of the slice: x: 4, y: 4, z: 16 (z_hi: 4, z_lo: 4; z = z_hi * 4 + z_lo), core: 2. Of those that a mesh axis runs over, the one named last changes fastest.
Arguments:
- x_rows: bfloat16 [3, 1024, 5120], P(None, 'roll'), may hold values from -6 to 6
- query_base_rows: bfloat16 [3, 1024, 5120], P(None, 'roll', 'learn'), may hold values from -8 to 8
- k_base: bfloat16 [3, 1024, 1024], P(None, 'roll', 'learn'), may hold values from -6 to 6
- value_base_rows: bfloat16 [3, 1024, 1024], P(None, 'roll', 'learn'), may hold values from -6 to 6
- k_pool: bfloat16 [2048, 128, 1024], P('roll', None, 'learn'), may hold values from -8 to 8
- v_pool: bfloat16 [2048, 128, 1024], P('roll', None, 'learn'), may hold values from -6 to 6
- block_dest: int32 [2048, 1], P('roll'), may hold values from 0 to 63; in each aligned block of 32 rows (0 to 31, 32 to 63, ...) no two rows name the same one
- block_slot: int32 [2048], P('roll'), may hold values from 0 to 15
- block_fill: int32 [2048], P('roll'), may hold values from 2 to 128, as said below
- a_query: bfloat16 [5120, 64], P('learn'), may hold values from -0.078125 to 0.078125
- query_up_factor: bfloat16 [64, 5120], P(None, 'learn'), may hold values from -0.75 to 0.75
- a_value: bfloat16 [5120, 64], P('learn'), may hold values from -0.078125 to 0.078125
- value_up_factor: bfloat16 [64, 1024], P(None, 'learn'), may hold values from -0.75 to 0.75
Outputs:
- attended: bfloat16 [3, 1024, 5120], P(None, 'roll', 'learn')
The draws below stay inside these ranges and needn't reach their ends.
Inputs may be any that keep to these rules, and one draw needn't show every extreme that they name: `block_dest`: within the 32 blocks of one index of roll at most 1 have the same owner, and some owner gets exactly 1 of them. `block_fill`: the live tokens of a block are its first ones; some block of every index of roll is full.
All inputs are finite; a program needn't handle non-finite values.
Results may differ from the reference program's by a relative error of at most 0.0051.
Values may be sent and summed in bfloat16 or wider, within the bound.
A program may use at most 64 MiB of HBM per device.

```python
import math
import jax
import jax.numpy as jnp
import numpy as np
from jax import lax

D = 5120
QH = 40
KVH = 8
HD = 128
RANK = 64
BLK = 128
STEPS = 3
POOL = 32
SLOTS = 16
CAP = 1
GROUP = 5
ROLLS = 1024
BLOCKS = 2048
N_ROLL = 64


def draw_k_pool(key, part):
    key = jax.random.fold_in(key, 7)
    array_shape = (BLOCKS, BLK, KVH, HD)
    base = jnp.clip(jax.random.normal(key, array_shape, jnp.float32), -8.0, 8.0)
    return base.reshape(BLOCKS, BLK, KVH * HD).astype(jnp.bfloat16)


def draw_query_base_rows(key, part):
    key = jax.random.fold_in(key, 11)
    key_base = jax.random.fold_in(key, 0)
    array_shape = (STEPS, ROLLS, QH, HD)
    base = jnp.clip(jax.random.normal(key_base, array_shape, jnp.float32), -8.0, 8.0)
    return base.reshape(STEPS, ROLLS, QH * HD).astype(jnp.bfloat16)


def draw_block_fill(key, part):
    key = jax.random.fold_in(key, 5)
    key_len, key_full = jax.random.split(key)
    partial_len = jax.random.randint(key_len, (BLOCKS,), 2, BLK + 1)
    full = jax.random.randint(key_full, (BLOCKS,), 0, 4) < 3
    first = jnp.arange(BLOCKS, dtype=jnp.int32) % POOL == 0
    return jnp.where(full | first, BLK, partial_len).astype(jnp.int32)


def set_ends(values, stream_key, smallest, high):
    longest = values.shape.index(max(values.shape))
    spots = []
    for shift in (0, 1):
        where = [jax.random.randint(jax.random.fold_in(stream_key, axis), (), 0, length) for axis, length in enumerate(values.shape)]
        where[longest] = (where[longest] + shift) % values.shape[longest]
        spots.append(tuple(where))
    return values.at[spots[0]].set(smallest).at[spots[1]].set(high)


def block_levels(rng, dims, pieces, low, top_value):
    factor_of = 1.0
    for position, shards_of in pieces:
        draws = jax.random.uniform(jax.random.fold_in(jax.random.fold_in(rng, 6), position), (shards_of,), jnp.float32, low / len(pieces), top_value / len(pieces))
        factor_of = factor_of * jnp.repeat(jnp.exp(draws), dims[position] // shards_of).reshape((-1,) + (1,) * (len(dims) - 1 - position))
    return factor_of


def shared_out(stream_key, own, number, rows, count, top, limit, skew):
    sequence = jax.random.permutation(stream_key, count)
    crowded, common = shares(count, rows * top, limit, skew, True), shares(count, rows * top, limit, skew, False)
    places = jnp.arange(count)

    def named(lengths, offset_by):
        used = int((lengths > 0).sum())
        fixed = max(1, used // 4)
        passed = fixed + (places - fixed + offset_by * (used - fixed)) % max(1, count - fixed)
        return jnp.zeros((count,), jnp.int32).at[sequence[jnp.where(places < fixed, places, passed)]].set(jnp.asarray(lengths, jnp.int32))

    lengths = jnp.where(number % 4 == 0, named(crowded, number // 4), named(common, number - number // 4 - 1))
    mixed = jax.random.permutation(jax.random.fold_in(own, 3), count)
    donor, sink = mixed[0:count // 2 * 2:2], mixed[1:count // 2 * 2:2]
    margin = jnp.minimum(lengths[donor] - 1, limit - lengths[sink]) // 2
    margin = jnp.where((donor == sequence[0]) | (sink == sequence[0]) | (lengths[sink] == 0), 0, jnp.maximum(margin, 0))
    passed = jax.random.randint(jax.random.fold_in(own, 4), (count // 2,), 0, 1 << 20) % (margin + 1)
    lengths = lengths.at[donor].add(-passed).at[sink].add(passed)
    items = jnp.searchsorted(jnp.cumsum(lengths), jnp.arange(rows * top), side="right").astype(jnp.int32)
    listing = items.reshape(top, rows).T
    listing = listing[jax.random.permutation(jax.random.fold_in(own, 1), rows)]
    offset_by = jax.random.randint(jax.random.fold_in(own, 2), (rows, 1), 0, top)
    return jnp.take_along_axis(listing, (jnp.arange(top)[None, :] + offset_by) % top, axis=1)


def shares(amount, total, reach, lean, full):
    weights = [(1 << 20) // math.isqrt(grade ** lean) + 1 for grade in range(1, amount + 1)]
    largest = reach if full else min(reach, max(-(-total // amount), total * weights[0] // sum(weights)))
    least = 1 if total - largest >= amount - 1 else 0
    holding, spare = [largest] + [least] * (amount - 1), total - largest - least * (amount - 1)
    while spare > 0:
        candidates = [i for i in range(1, amount) if holding[i] < largest] or [i for i in range(1, amount) if holding[i] < reach]
        pool, left = sum([weights[i] for i in candidates]), spare
        for i in candidates:
            more = min(reach - holding[i], max(1, left * weights[i] // pool), spare)
            holding[i] = holding[i] + more
            spare = spare - more
    return np.array(holding)


def noise(key, extent, spread, limit, cuts=(), kind=jnp.bfloat16):
    values = jax.random.normal(key, extent, jnp.float32) * spread
    if len(cuts) > 0:
        values = block_levels(key, extent, cuts, -0.22, 0.18) * values
    return jnp.clip(values, min=-limit, max=limit).astype(kind)


def setup_inputs(seed: int = 0) -> dict:
    key_list = jax.random.split(jax.random.key(seed), 14)
    x_rows = noise(key_list[0], (STEPS, ROLLS, D), 1.0, 6.0, ((1, 64),))
    query_base_rows = draw_query_base_rows(jax.random.fold_in(key_list[13], 71), 0)
    k_base = noise(key_list[2], (STEPS, ROLLS, KVH * HD), 1.0, 6.0, ((1, 64), (2, 8)))
    value_base_rows = noise(key_list[3], (STEPS, ROLLS, KVH * HD), 1.0, 6.0, ((1, 64), (2, 8)))
    k_pool = draw_k_pool(jax.random.fold_in(key_list[13], 71), 0)
    v_pool = noise(key_list[5], (BLOCKS, BLK, KVH * HD), 1.0, 6.0, ((0, 64), (2, 8)))
    block_dest_keys = jax.random.split(jax.random.fold_in(key_list[6], 1), BLOCKS // POOL)
    block_dest_turns = jax.random.permutation(jax.random.fold_in(key_list[6], 3), BLOCKS // POOL)
    block_dest = jax.vmap(lambda own, number: shared_out(jax.random.fold_in(key_list[6], 2), own, number, POOL, N_ROLL, 1, CAP, 2))(block_dest_keys, block_dest_turns).reshape((BLOCKS, 1))
    block_slot = set_ends(jax.random.randint(key_list[7], (BLOCKS,), 0, SLOTS), jax.random.fold_in(key_list[7], 1), 0, SLOTS - 1).astype(jnp.int32)
    block_fill = draw_block_fill(jax.random.fold_in(key_list[13], 71), 0)
    a_query = noise(key_list[9], (D, RANK), D ** -0.5, 0.078125, ((0, 8),))
    query_up_factor = noise(key_list[10], (RANK, QH * HD), RANK ** -0.5, 0.75, ((1, 8),))
    a_value = noise(key_list[11], (D, RANK), D ** -0.5, 0.078125, ((0, 8),))
    value_up_factor = noise(key_list[12], (RANK, KVH * HD), RANK ** -0.5, 0.75, ((1, 8),))
    return {"x_rows": x_rows, "query_base_rows": query_base_rows, "k_base": k_base, "value_base_rows": value_base_rows, "k_pool": k_pool, "v_pool": v_pool, "block_dest": block_dest, "block_slot": block_slot, "block_fill": block_fill, "a_query": a_query, "query_up_factor": query_up_factor, "a_value": a_value, "value_up_factor": value_up_factor}


adapter_scale = 0.5
masked_score = -1e+30

def block_partials(queries, keys, values, fill):
    scores = jnp.einsum('nkqd,njkd->nkqj', queries.astype(jnp.float32), keys.astype(jnp.float32)) / math.sqrt(HD)
    live = jnp.arange(keys.shape[1], dtype=jnp.int32)[None, None, None, :] < fill[:, None, None, None]
    scores = jnp.where(live, scores, masked_score)
    peak = lax.optimization_barrier(jnp.max(scores, axis=3))
    weights = jnp.where(live, jnp.exp(scores - peak[..., None]), 0.0)
    total = lax.optimization_barrier(jnp.sum(weights, axis=3))
    mixed = jnp.einsum('nkqj,njkd->nkqd', weights.astype(jnp.bfloat16).astype(jnp.float32), values.astype(jnp.float32))
    return (peak, total, mixed)

def new_partials(queries, keys, values):
    scores = jnp.einsum('skqd,uskd->skqu', queries.astype(jnp.float32), keys.astype(jnp.float32)) / math.sqrt(HD)
    row_step = jnp.arange(STEPS * GROUP, dtype=jnp.int32) // GROUP
    live = jnp.arange(STEPS, dtype=jnp.int32)[None, :] <= row_step[:, None]
    scores = jnp.where(live[None, None], scores, masked_score)
    peak = lax.optimization_barrier(jnp.max(scores, axis=3))
    weights = jnp.where(live[None, None], jnp.exp(scores - peak[..., None]), 0.0)
    total = lax.optimization_barrier(jnp.sum(weights, axis=3))
    mixed = jnp.einsum('skqu,uskd->skqd', weights.astype(jnp.bfloat16).astype(jnp.float32), values.astype(jnp.float32))
    return (peak, total, mixed)

def reference(x_rows, query_base_rows, k_base, value_base_rows, k_pool, v_pool, block_dest, block_slot, block_fill, a_query, query_up_factor, a_value, value_up_factor):
    flat = x_rows.reshape(STEPS * ROLLS, D)
    query_down_product = jnp.dot(flat, a_query, preferred_element_type=jnp.float32).astype(jnp.bfloat16)
    value_down_product = jnp.dot(flat, a_value, preferred_element_type=jnp.float32).astype(jnp.bfloat16)
    query_vectors = query_base_rows.astype(jnp.float32) + adapter_scale * jnp.dot(query_down_product, query_up_factor, preferred_element_type=jnp.float32).reshape(query_base_rows.shape)
    query_vectors = query_vectors.astype(jnp.bfloat16)
    fresh_value_rows = value_base_rows.astype(jnp.float32) + adapter_scale * jnp.dot(value_down_product, value_up_factor, preferred_element_type=jnp.float32).reshape(value_base_rows.shape)
    fresh_value_rows = fresh_value_rows.astype(jnp.bfloat16)
    q_roll = query_vectors.reshape(STEPS, ROLLS, KVH, GROUP, HD).transpose(1, 2, 0, 3, 4).reshape(ROLLS, KVH, STEPS * GROUP, HD)
    key_new = k_base.reshape(STEPS, ROLLS, KVH, HD)
    value_rows = fresh_value_rows.reshape(STEPS, ROLLS, KVH, HD)
    peak_new, total_new, mixed_new = new_partials(q_roll, key_new, value_rows)
    owner = (block_dest[:, 0] * SLOTS + block_slot).astype(jnp.int32)
    keys = k_pool.reshape(BLOCKS, BLK, KVH, HD)
    values = v_pool.reshape(BLOCKS, BLK, KVH, HD)

    def one_head(head):
        q_head = lax.dynamic_slice_in_dim(q_roll, head, 1, 1)[owner]
        k_head = lax.dynamic_slice_in_dim(keys, head, 1, 2)
        v_head = lax.dynamic_slice_in_dim(values, head, 1, 2)
        return block_partials(q_head, k_head, v_head, block_fill)
    peak, total, mixed = lax.map(one_head, jnp.arange(KVH, dtype=jnp.int32))
    peak = peak[:, :, 0].transpose(1, 0, 2)
    total = total[:, :, 0].transpose(1, 0, 2)
    mixed = mixed[:, :, 0].transpose(1, 0, 2, 3)
    block_peak = jax.ops.segment_max(peak, owner, num_segments=ROLLS)
    top = jnp.maximum(block_peak, peak_new)
    weight = jnp.exp(peak - top[owner])
    total_all = total_new * jnp.exp(peak_new - top) + jax.ops.segment_sum(weight * total, owner, num_segments=ROLLS)
    mixed_all = mixed_new * jnp.exp(peak_new - top)[..., None] + jax.ops.segment_sum(weight[..., None] * mixed, owner, num_segments=ROLLS)
    result = mixed_all / total_all[..., None]
    result = result.reshape(ROLLS, KVH, STEPS, GROUP, HD).transpose(2, 0, 1, 3, 4).reshape(STEPS, ROLLS, QH * HD)
    return result.astype(jnp.bfloat16)
```

```python
import functools
import math

import jax
import jax.numpy as jnp
from jax import lax
from jax.experimental import pallas as pl
from jax.experimental.pallas import tpu as pltpu
from jax.sharding import PartitionSpec as P

MESH = pl.DeviceIdType.MESH
F32 = jnp.float32
BF16 = jnp.bfloat16
HD = 128
ROWS = 16
adapter_scale = 0.5
masked_score = -1e30
no_slot = -1000.0


def iota(shape, dim):
    return lax.broadcasted_iota(jnp.int32, shape, dim)


def diagonal(column):
    n = column.shape[0]
    here = iota((n, HD), 1) == lax.rem(iota((n, HD), 0), ROWS)
    spread = jnp.where(here, jnp.broadcast_to(column, (n, HD)), 0.0)
    return jnp.sum(spread.reshape(n // ROWS, ROWS, HD), axis=1)


def kernel(
    peers,
    ranks,
    dims,
    x_hbm,
    qb_hbm,
    kb_hbm,
    vb_hbm,
    kp_hbm,
    vp_hbm,
    dest,
    slot,
    fill,
    aq_hbm,
    qu_hbm,
    av_hbm,
    vu_hbm,
    out_ref,
    x,
    qb,
    kb,
    vb,
    kp,
    vp,
    aq,
    qu,
    av,
    vu,
    tag_send,
    tag_recv,
    lane_vec,
    lane_blk,
    lq_recv,
    lv_recv,
    tagc,
    sel,
    sel_t,
    q_send,
    q_recv,
    part,
    lse_blk,
    p_send,
    p_recv,
    l_send,
    l_recv,
    new_mixed,
    top_s,
    den_s,
    wide,
    weighted,
    local_sem,
    blk_sem,
    send_sem,
    recv_sem,
    low_send_sem,
    low_recv_sem,
):
    steps, slots, chunk, pool, block_len, group = dims
    rows = steps * group
    me, ml = lax.axis_index("roll"), lax.axis_index("learn")
    others = pl.ds(0, peers - 1)

    barrier = pltpu.get_barrier_semaphore()

    def greet(i, carry):
        pl.semaphore_signal(
            barrier, inc=1, device_id=(lax.rem(me + i, peers), ml), device_id_type=MESH
        )
        return carry

    lax.fori_loop(1, peers, greet, 0)
    for i in range(1, ranks):
        pl.semaphore_signal(
            barrier, inc=1, device_id=(me, lax.rem(ml + i, ranks)), device_id_type=MESH
        )

    start = pl.multiple_of(ml * chunk, HD)
    pairs = [
        (x_hbm.at[:, :, pl.ds(start, chunk)], x),
        (aq_hbm, aq),
        (av_hbm, av),
        (qb_hbm, qb),
        (qu_hbm, qu),
        (kb_hbm, kb),
        (vb_hbm, vb),
        (vu_hbm, vu),
        (kp_hbm, kp),
        (vp_hbm, vp),
    ]
    loads = [pltpu.make_async_copy(a, b, local_sem.at[i]) for i, (a, b) in enumerate(pairs)]
    for load in loads:
        load.start()

    lane = iota((1, HD), 1)
    tag_row = jnp.full((1, HD), no_slot, F32)
    blk_row = jnp.zeros((1, HD), jnp.int32)
    for b in range(pool):
        hit = lane == dest[b, 0]
        tag_row = jnp.where(hit, slot[b].astype(F32), tag_row)
        blk_row = jnp.where(hit, b, blk_row)
    tag_send[...] = tag_row
    tag_recv[pl.ds(me, 1), :] = tag_row
    lane_vec[...] = blk_row
    to_smem = pltpu.make_async_copy(lane_vec, lane_blk, blk_sem)
    to_smem.start()

    for load in loads[:3]:
        load.wait()
    x_rows = x[...].reshape(steps * slots, chunk)
    half = steps * slots // 2

    def packed(a):
        low = jnp.dot(x_rows, a[...], preferred_element_type=F32)
        return jnp.concatenate([low[:half], low[half:]], axis=1)

    lq_recv[ml] = packed(aq)
    lv_recv[ml] = packed(av)

    pl.semaphore_wait(barrier, peers + ranks - 2)

    def to_learn(buf, k):
        copies = []
        for i in range(1, ranks):
            copies.append(
                pltpu.make_async_remote_copy(
                    src_ref=buf.at[ml],
                    dst_ref=buf.at[ml],
                    send_sem=low_send_sem.at[k],
                    recv_sem=low_recv_sem.at[k],
                    device_id=(me, lax.rem(ml + i, ranks)),
                    device_id_type=MESH,
                )
            )
            copies[-1].start()

    to_learn(lq_recv, 0)

    def to_roll(src_of, dst, k):
        def one(i, carry):
            d = lax.rem(me + i, peers)
            pltpu.make_async_remote_copy(
                src_ref=src_of(d),
                dst_ref=dst,
                send_sem=send_sem.at[k],
                recv_sem=recv_sem.at[k],
                device_id=(d, ml),
                device_id_type=MESH,
            ).start()
            return carry

        lax.fori_loop(1, peers, one, 0)

    to_roll(lambda d: tag_send, tag_recv.at[pl.ds(me, 1), :], 0)
    to_learn(lv_recv, 1)

    def wait_lanes(buf, sem):
        pltpu.make_async_copy(buf.at[others], buf.at[others], sem).wait()

    def wait_learn(buf, sem):
        rest = buf.at[pl.ds(0, ranks - 1)]
        pltpu.make_async_copy(rest, rest, sem).wait()

    wait_lanes(tag_recv, recv_sem.at[0])
    mine = iota((peers, HD), 1) == me
    asked = jnp.sum(jnp.where(mine, tag_recv[...], 0.0), axis=1, keepdims=True)
    tagc[...] = jnp.broadcast_to(asked, (peers, HD))

    width = ROWS * slots
    sel_row = (iota((ROWS, width), 0) * slots).astype(F32)
    sel_lane = iota((ROWS, width), 1).astype(F32)

    def pick(l, carry):
        row = tagc[pl.ds(l, 1), :]
        want = sel_row + jnp.concatenate([row] * (width // HD), axis=1)
        hot = jnp.where(want == sel_lane, 1.0, 0.0).astype(BF16)
        sel[pl.ds(pl.multiple_of(l * ROWS, ROWS), ROWS), :] = hot
        return carry

    lax.fori_loop(0, peers, pick, 0, unroll=8)

    def unpacked(buf):
        low = buf[0]
        for i in range(1, ranks):
            low = low + buf[i]
        rank = low.shape[1] // 2
        return jnp.concatenate([low[:, :rank], low[:, rank:]], axis=0).astype(BF16)

    for load in loads[3:5]:
        load.wait()
    wait_learn(lq_recv, low_recv_sem.at[0])
    up = jnp.dot(unpacked(lq_recv), qu[...], preferred_element_type=F32)
    query = qb[...].reshape(steps * slots, group * HD).astype(F32) + adapter_scale * up
    query = query.astype(BF16)
    tiles = [
        query[t * slots : (t + 1) * slots, g * HD : (g + 1) * HD]
        for t in range(steps)
        for g in range(group)
    ]
    stack = jnp.concatenate(tiles + [jnp.zeros((slots, HD), BF16)] * (ROWS - rows), axis=0)
    picked = jnp.dot(sel[...], stack, preferred_element_type=F32).astype(BF16)
    q_send[...] = picked.reshape(peers, ROWS, HD)
    q_recv[me] = q_send[me]
    to_roll(lambda d: q_send.at[d], q_recv.at[me], 1)

    sel_t[...] = sel[...].T
    for load in loads[5:8]:
        load.wait()
    wait_learn(lv_recv, low_recv_sem.at[1])
    up_v = jnp.dot(unpacked(lv_recv), vu[...], preferred_element_type=F32)
    value = vb[...].reshape(steps * slots, HD).astype(F32) + adapter_scale * up_v
    value = value.astype(BF16).astype(F32)
    values = [value[t * slots : (t + 1) * slots] for t in range(steps)]
    keys = [kb[t].astype(F32) for t in range(steps)]
    scale = 1.0 / math.sqrt(HD)
    lane_s = iota((slots, HD), 1)
    scores = [jnp.full((slots, HD), masked_score, F32) for _ in range(steps)]
    for r in range(rows):
        q_r = tiles[r].astype(F32)
        for u in range(r // group + 1):
            s = jnp.sum(q_r * keys[u], axis=1, keepdims=True) * scale
            scores[u] = jnp.where(lane_s == r, s, scores[u])
    new_peak = functools.reduce(jnp.maximum, scores)
    new_w = [
        jnp.where(lane_s >= u * group, jnp.exp(scores[u] - new_peak), 0.0) for u in range(steps)
    ]
    new_total = functools.reduce(jnp.add, new_w)
    rounded = [w.astype(BF16).astype(F32) for w in new_w]
    for r in range(rows):
        acc = jnp.zeros((slots, HD), F32)
        for u in range(r // group + 1):
            acc = acc + rounded[u][:, r : r + 1] * values[u]
        new_mixed[pl.ds(r * slots, slots), :] = acc

    for load in loads[8:]:
        load.wait()
    to_smem.wait()
    wait_lanes(q_recv, recv_sem.at[1])
    batch = 8
    token = iota((ROWS, block_len), 1)

    def some_blocks(i, carry):
        scored = []
        for j in range(batch):
            b = i * batch + j
            s = lax.dot_general(
                q_recv[dest[b, 0]], kp[b], (((1,), (1,)), ((), ())), preferred_element_type=F32
            )
            scored.append(jnp.where(token < fill[b], s * scale, masked_score))
        s = jnp.concatenate(scored, axis=0)
        peak = jnp.max(s, axis=1, keepdims=True)
        w = jnp.exp(s - peak)
        total = jnp.sum(w, axis=1, keepdims=True)
        w16 = w.astype(BF16)
        mixed = jnp.concatenate(
            [
                jnp.dot(w16[j * ROWS : (j + 1) * ROWS], vp[i * batch + j], preferred_element_type=F32)
                for j in range(batch)
            ],
            axis=0,
        )
        first = pl.multiple_of(i * batch, batch)
        part[pl.ds(first, batch)] = (mixed / total).astype(BF16).reshape(batch, ROWS, HD)
        lse_blk[pl.ds(first, batch), :] = diagonal(peak + jnp.log(total))
        return carry

    lax.fori_loop(0, pool // batch, some_blocks, 0)

    def to_lane(l, carry):
        b = lane_blk[0, l]
        p_send[l] = part[b]
        l_send[pl.ds(l, 1), :] = lse_blk[pl.ds(b, 1), :]
        return carry

    lax.fori_loop(0, peers, to_lane, 0, unroll=8)
    p_recv[me] = p_send[me]
    l_recv[pl.ds(me, 1), :] = l_send[pl.ds(me, 1), :]
    to_roll(lambda d: p_send.at[d], p_recv.at[me], 2)
    to_roll(lambda d: l_send.at[pl.ds(d, 1), :], l_recv.at[pl.ds(me, 1), :], 3)

    wait_lanes(l_recv, recv_sem.at[3])
    tags = tagc[...]
    lse = jnp.where(tags >= 0.0, l_recv[...], masked_score)
    for s in range(slots):
        mine_s = jnp.where(tags == float(s), lse, masked_score)
        top_s[pl.ds(s, 1), :] = jnp.max(mine_s, axis=0, keepdims=True)
    top = jnp.maximum(top_s[...], new_peak)
    top_s[...] = top
    lane_top = jnp.zeros((peers, HD), F32)
    for s in range(slots):
        lane_top = jnp.where(tags == float(s), top_s[pl.ds(s, 1), :], lane_top)
    weight = jnp.exp(lse - lane_top)
    for s in range(slots):
        mine_s = jnp.where(tags == float(s), weight, 0.0)
        den_s[pl.ds(s, 1), :] = jnp.sum(mine_s, axis=0, keepdims=True)
    new_weight = jnp.exp(new_peak - top)
    inverse = 1.0 / (den_s[...] + new_total * new_weight)
    den_s[...] = inverse
    lane_inv = jnp.zeros((peers, HD), F32)
    for s in range(slots):
        lane_inv = jnp.where(tags == float(s), den_s[pl.ds(s, 1), :], lane_inv)
    wide[...] = weight * lane_inv
    new_share = new_weight * inverse

    wait_lanes(p_recv, recv_sem.at[2])
    on_row = iota((ROWS, HD), 0) == iota((ROWS, HD), 1)

    def weigh(l, carry):
        row = jnp.where(on_row, wide[pl.ds(l, 1), :], 0.0)
        column = jnp.sum(row, axis=1, keepdims=True)
        at = pl.ds(pl.multiple_of(l * ROWS, ROWS), ROWS)
        weighted[at, :] = (p_recv[l].astype(F32) * column).astype(BF16)
        return carry

    lax.fori_loop(0, peers, weigh, 0, unroll=8)
    mixed = jnp.dot(sel_t[...], weighted[...], preferred_element_type=F32)
    for r in range(rows):
        t, g = r // group, r % group
        at = slice(r * slots, (r + 1) * slots)
        res = mixed[at] + new_share[:, r : r + 1] * new_mixed[at, :]
        out_ref[t, :, g * HD : (g + 1) * HD] = res.astype(BF16)

    wait_learn(lq_recv, low_send_sem.at[0])
    wait_learn(lv_recv, low_send_sem.at[1])
    wait_lanes(tag_recv, send_sem.at[0])
    wait_lanes(q_recv, send_sem.at[1])
    wait_lanes(p_recv, send_sem.at[2])
    wait_lanes(l_recv, send_sem.at[3])


def on_device(
    x_rows,
    query_base_rows,
    k_base,
    value_base_rows,
    k_pool,
    v_pool,
    block_dest,
    block_slot,
    block_fill,
    a_query,
    query_up_factor,
    a_value,
    value_up_factor,
):
    peers, ranks = lax.axis_size("roll"), lax.axis_size("learn")
    steps, slots, width = x_rows.shape
    pool, block_len, _ = k_pool.shape
    rank = a_query.shape[1]
    group = query_base_rows.shape[2] // HD
    chunk = width // ranks
    half = steps * slots // 2
    dims = (steps, slots, chunk, pool, block_len, group)
    hbm = pl.BlockSpec(memory_space=pltpu.HBM)
    smem = pl.BlockSpec(memory_space=pltpu.SMEM)
    vmem = pltpu.VMEM
    dma = pltpu.SemaphoreType.DMA
    return pl.pallas_call(
        functools.partial(kernel, peers, ranks, dims),
        out_shape=jax.ShapeDtypeStruct(query_base_rows.shape, BF16),
        in_specs=[hbm] * 6 + [smem] * 3 + [hbm] * 4,
        out_specs=pl.BlockSpec(memory_space=pltpu.VMEM),
        scratch_shapes=[
            vmem((steps, slots, chunk), BF16),
            vmem(query_base_rows.shape, BF16),
            vmem(k_base.shape, BF16),
            vmem(value_base_rows.shape, BF16),
            vmem(k_pool.shape, BF16),
            vmem(v_pool.shape, BF16),
            vmem(a_query.shape, BF16),
            vmem(query_up_factor.shape, BF16),
            vmem(a_value.shape, BF16),
            vmem(value_up_factor.shape, BF16),
            vmem((1, HD), F32),
            vmem((peers, HD), F32),
            vmem((1, HD), jnp.int32),
            pltpu.SMEM((1, HD), jnp.int32),
            vmem((ranks, half, 2 * rank), F32),
            vmem((ranks, half, 2 * rank), F32),
            vmem((peers, HD), F32),
            vmem((peers * ROWS, ROWS * slots), BF16),
            vmem((ROWS * slots, peers * ROWS), BF16),
            vmem((peers, ROWS, HD), BF16),
            vmem((peers, ROWS, HD), BF16),
            vmem((pool, ROWS, HD), BF16),
            vmem((pool, HD), F32),
            vmem((peers, ROWS, HD), BF16),
            vmem((peers, ROWS, HD), BF16),
            vmem((peers, HD), F32),
            vmem((peers, HD), F32),
            vmem((ROWS * slots, HD), F32),
            vmem((slots, HD), F32),
            vmem((slots, HD), F32),
            vmem((peers, HD), F32),
            vmem((peers * ROWS, HD), BF16),
            dma((10,)),
            dma,
            dma((4,)),
            dma((4,)),
            dma((2,)),
            dma((2,)),
        ],
        compiler_params=pltpu.CompilerParams(
            collective_id=0, has_side_effects=True, vmem_limit_bytes=48 * 1024 * 1024
        ),
    )(
        x_rows,
        query_base_rows,
        k_base,
        value_base_rows,
        k_pool,
        v_pool,
        block_dest,
        block_slot,
        block_fill,
        a_query,
        query_up_factor,
        a_value,
        value_up_factor,
    )


def solution(mesh):
    return jax.shard_map(
        on_device,
        mesh=mesh,
        in_specs=(
            P(None, "roll", None),
            P(None, "roll", "learn"),
            P(None, "roll", "learn"),
            P(None, "roll", "learn"),
            P("roll", None, "learn"),
            P("roll", None, "learn"),
            P("roll", None),
            P("roll"),
            P("roll"),
            P("learn", None),
            P(None, "learn"),
            P("learn", None),
            P(None, "learn"),
        ),
        out_specs=P(None, "roll", "learn"),
        check_vma=False,
    )
```

```python
import functools
import math

import jax
import jax.numpy as jnp
from jax import lax
from jax.experimental import pallas as pl
from jax.experimental.pallas import tpu as pltpu
from jax.sharding import PartitionSpec as P

MESH = pl.DeviceIdType.MESH
F32 = jnp.float32
BF16 = jnp.bfloat16
HD = 128
ROWS = 16
adapter_scale = 0.5
masked_score = -1e30
no_slot = -1000.0


def iota(shape, dim):
    return lax.broadcasted_iota(jnp.int32, shape, dim)


def in_spare_row(column, tiles):
    n = column.shape[0]
    row, lane = lax.rem(iota((n, HD), 0), ROWS), iota((n, HD), 1)
    high = column.astype(BF16).astype(F32)
    middle = (column - high).astype(BF16).astype(F32)
    low = column - high - middle
    spread = jnp.where(lane == row, high, 0.0)
    spread = jnp.where(lane == row + ROWS, middle, spread)
    spread = jnp.where(lane == row + 2 * ROWS, low, spread)
    line = jnp.sum(spread.reshape(n // ROWS, ROWS, HD), axis=1, keepdims=True)
    tiles = tiles.reshape(n // ROWS, ROWS, HD)
    return jnp.where(iota(tiles.shape, 1) == ROWS - 1, line, tiles)


def kernel(
    peers,
    ranks,
    dims,
    x_hbm,
    qb_hbm,
    kb_hbm,
    vb_hbm,
    kp_hbm,
    vp_hbm,
    dest,
    slot,
    fill,
    aq_hbm,
    qu_hbm,
    av_hbm,
    vu_hbm,
    out_ref,
    x,
    qb,
    kb,
    vb,
    kp,
    vp,
    a_both,
    qu,
    vu,
    tag_send,
    tag_recv,
    lane_vec,
    lane_blk,
    low_recv,
    low_total,
    tagc,
    sel,
    sel_t,
    q_send,
    q_recv,
    part,
    p_send,
    p_recv,
    new_mixed,
    top_s,
    den_s,
    wide,
    weighted,
    local_sem,
    blk_sem,
    send_sem,
    recv_sem,
    low_send_sem,
    low_recv_sem,
    inner_in,
    roll_in,
):
    steps, slots, chunk, pool, block_len, group = dims
    rows = steps * group
    rank = aq_hbm.shape[0]
    me, ml = lax.axis_index("roll"), lax.axis_index("learn")
    others = pl.ds(0, peers - 1)

    chips = ranks // 2
    chip, core = ml // 2, lax.rem(ml, 2)
    partner = ml + 1 - 2 * core
    is_inner, is_outer = chip < 2, chip >= 2
    is_outer0 = jnp.logical_and(is_outer, core == 0)
    is_outer1 = jnp.logical_and(is_outer, core == 1)
    n_inner = 4
    barrier = pltpu.get_barrier_semaphore()
    gatherer = ml - core * (chip // 2)

    start = pl.multiple_of(ml * chunk, HD)
    pairs = [
        (x_hbm.at[:, :, pl.ds(start, chunk)], x),
        (aq_hbm, a_both.at[pl.ds(0, rank)]),
        (av_hbm, a_both.at[pl.ds(rank, rank)]),
        (qb_hbm, qb),
        (qu_hbm, qu),
        (kb_hbm, kb),
        (vb_hbm, vb),
        (vu_hbm, vu),
        (kp_hbm, kp),
        (vp_hbm, vp),
    ]
    loads = [pltpu.make_async_copy(a, b, local_sem.at[i]) for i, (a, b) in enumerate(pairs)]
    for load in loads[:3]:
        load.start()

    def signal(sem, roll, learn):
        pl.semaphore_signal(sem, inc=1, device_id=(roll, learn), device_id_type=MESH)

    def greet(i, carry):
        signal(barrier, lax.rem(me + i, peers), gatherer)
        return carry

    signal(barrier, me, partner)

    @pl.when(is_inner)
    def _():
        signal(barrier, me, 2 - 2 * chip)
        signal(barrier, me, 3 - 2 * chip)
        for j in range(2, chips):
            signal(barrier, me, 2 * j + 1)

    @pl.when(is_inner)
    def _():
        lax.fori_loop(1, peers, greet, 0, unroll=7)

    for load in loads[3:]:
        load.start()

    for load in loads[:3]:
        load.wait()
    partial = lax.dot_general(
        x[...].reshape(steps * slots, chunk),
        a_both[...],
        (((1,), (1,)), ((), ())),
        preferred_element_type=F32,
    )
    low_recv[ml] = partial.astype(BF16)

    def to_learn(src, dst, k, learn):
        return pltpu.make_async_remote_copy(
            src_ref=src,
            dst_ref=dst,
            send_sem=low_send_sem.at[k],
            recv_sem=low_recv_sem.at[k],
            device_id=(me, learn),
            device_id_type=MESH,
        )

    @pl.when(is_inner)
    def _():
        pl.semaphore_wait(barrier, peers + 2)

    @pl.when(is_outer1)
    def _():
        pl.semaphore_wait(barrier, n_inner + 1)
        signal(inner_in, me, partner)

    @pl.when(is_outer0)
    def _():
        pl.semaphore_wait(inner_in, 1)

    mine = low_recv.at[ml]

    @pl.when(is_inner)
    def _():
        to_learn(mine, mine, 0, partner).start()
        to_learn(mine, mine, 0, 2 - 2 * chip).start()
        to_learn(mine, mine, 0, 3 - 2 * chip).start()

    @pl.when(is_outer)
    def _():
        for j in range(n_inner):
            to_learn(mine, mine, 0, j).start()

    @pl.when(is_outer)
    def _():
        lax.fori_loop(1, peers, greet, 0, unroll=7)

    lane = iota((1, HD), 1)
    tag_row = jnp.full((1, HD), no_slot, F32)
    blk_row = jnp.zeros((1, HD), jnp.int32)
    for b in range(pool):
        hit = lane == dest[0, b]
        tag_row = jnp.where(hit, slot[b].astype(F32), tag_row)
        blk_row = jnp.where(hit, b, blk_row)
    tag_send[...] = tag_row
    tag_recv[pl.ds(me, 1), :] = tag_row
    lane_vec[...] = blk_row
    to_smem = pltpu.make_async_copy(lane_vec, lane_blk, blk_sem)
    to_smem.start()

    @pl.when(is_outer0)
    def _():
        pl.semaphore_wait(barrier, 2 * peers - 1)
        signal(roll_in, me, partner)

    @pl.when(is_outer1)
    def _():
        pl.semaphore_wait(roll_in, 1)

    def to_roll(src_of, dst, k):
        def one(i, carry):
            d = lax.rem(me + i, peers)
            pltpu.make_async_remote_copy(
                src_ref=src_of(d),
                dst_ref=dst,
                send_sem=send_sem.at[k],
                recv_sem=recv_sem.at[k],
                device_id=(d, ml),
                device_id_type=MESH,
            ).start()
            return carry

        lax.fori_loop(1, peers, one, 0)

    to_roll(lambda d: tag_send, tag_recv.at[pl.ds(me, 1), :], 0)


    def wait_lanes(buf, sem):
        pltpu.make_async_copy(buf.at[others], buf.at[others], sem).wait()

    def wait_for(ref, sem):
        pltpu.make_async_copy(ref, ref, sem).wait()

    wait_lanes(tag_recv, recv_sem.at[0])
    mine = iota((peers, HD), 1) == me
    asked = jnp.sum(jnp.where(mine, tag_recv[...], 0.0), axis=1, keepdims=True)
    tagc[...] = jnp.broadcast_to(asked, (peers, HD))

    width = ROWS * slots
    sel_row = (iota((ROWS, width), 0) * slots).astype(F32)
    sel_lane = iota((ROWS, width), 1).astype(F32)

    def pick(l, carry):
        row = tagc[pl.ds(l, 1), :]
        want = sel_row + jnp.concatenate([row] * (width // HD), axis=1)
        hot = jnp.where(want == sel_lane, 1.0, 0.0).astype(BF16)
        sel[pl.ds(pl.multiple_of(l * ROWS, ROWS), ROWS), :] = hot
        return carry

    lax.fori_loop(0, peers, pick, 0, unroll=8)

    for load in loads[3:5]:
        load.wait()

    @pl.when(is_inner)
    def _():
        wait_for(low_recv.at[pl.ds(0, ranks - 1)], low_recv_sem.at[0])
        summed = functools.reduce(jnp.add, [low_recv[j].astype(F32) for j in range(ranks)])
        low_total[...] = summed.astype(BF16)
        to_learn(low_total, low_total, 1, 2 * (chips - 1 - chip) + core).start()

    @pl.when(is_outer)
    def _():
        wait_for(low_total, low_recv_sem.at[1])

    up = jnp.dot(low_total[:, :rank], qu[...], preferred_element_type=F32)
    query = qb[...].reshape(steps * slots, group * HD).astype(F32) + adapter_scale * up
    query = query.astype(BF16)
    tiles = [
        query[t * slots : (t + 1) * slots, g * HD : (g + 1) * HD]
        for t in range(steps)
        for g in range(group)
    ]
    stack = jnp.concatenate(tiles + [jnp.zeros((slots, HD), BF16)] * (ROWS - rows), axis=0)
    picked = jnp.dot(sel[...], stack, preferred_element_type=F32).astype(BF16)
    q_send[...] = picked.reshape(peers, ROWS, HD)
    q_recv[me] = q_send[me]
    to_roll(lambda d: q_send.at[d], q_recv.at[me], 1)

    sel_t[...] = sel[...].T

    for load in loads[8:]:
        load.wait()
    to_smem.wait()
    wait_lanes(q_recv, recv_sem.at[1])
    scale = 1.0 / math.sqrt(HD)
    batch = 8
    token = iota((ROWS, block_len), 1)

    def some_blocks(i, carry):
        scored = []
        for j in range(batch):
            b = i * batch + j
            s = lax.dot_general(
                q_recv[dest[0, b]], kp[b], (((1,), (1,)), ((), ())), preferred_element_type=F32
            )
            scored.append(jnp.where(token < fill[b], s * scale, masked_score))
        s = jnp.concatenate(scored, axis=0)
        peak = jnp.max(s, axis=1, keepdims=True)
        w = jnp.exp(s - peak)
        total = jnp.sum(w, axis=1, keepdims=True)
        w16 = w.astype(BF16)
        mixed = jnp.concatenate(
            [
                jnp.dot(w16[j * ROWS : (j + 1) * ROWS], vp[i * batch + j], preferred_element_type=F32)
                for j in range(batch)
            ],
            axis=0,
        )
        first = pl.multiple_of(i * batch, batch)
        tiles = in_spare_row(peak + jnp.log(total), mixed / total)
        part[pl.ds(first, batch)] = tiles.astype(BF16)
        return carry

    lax.fori_loop(0, pool // batch, some_blocks, 0)

    def to_lane(l, carry):
        p_send[l] = part[lane_blk[0, l]]
        return carry

    lax.fori_loop(0, peers, to_lane, 0, unroll=8)
    p_recv[me] = p_send[me]
    to_roll(lambda d: p_send.at[d], p_recv.at[me], 2)

    for load in loads[5:8]:
        load.wait()
    up_v = jnp.dot(low_total[:, rank:], vu[...], preferred_element_type=F32)
    value = vb[...].reshape(steps * slots, HD).astype(F32) + adapter_scale * up_v
    value = value.astype(BF16).astype(F32)
    values = [value[t * slots : (t + 1) * slots] for t in range(steps)]
    keys = [kb[t].astype(F32) for t in range(steps)]
    lane_s = iota((slots, HD), 1)
    scores = [jnp.full((slots, HD), masked_score, F32) for _ in range(steps)]
    for r in range(rows):
        q_r = tiles[r].astype(F32)
        for u in range(r // group + 1):
            s = jnp.sum(q_r * keys[u], axis=1, keepdims=True) * scale
            scores[u] = jnp.where(lane_s == r, s, scores[u])
    new_peak = functools.reduce(jnp.maximum, scores)
    new_w = [
        jnp.where(lane_s >= u * group, jnp.exp(scores[u] - new_peak), 0.0) for u in range(steps)
    ]
    new_total = functools.reduce(jnp.add, new_w)
    rounded = [w.astype(BF16).astype(F32) for w in new_w]
    for r in range(rows):
        acc = jnp.zeros((slots, HD), F32)
        for u in range(r // group + 1):
            acc = acc + rounded[u][:, r : r + 1] * values[u]
        new_mixed[pl.ds(r * slots, slots), :] = acc

    wait_lanes(p_recv, recv_sem.at[2])

    def spare_row(l, carry):
        wide[pl.ds(l, 1), :] = p_recv[l].astype(F32)[ROWS - 1 :]
        return carry

    lax.fori_loop(0, peers, spare_row, 0, unroll=8)
    tags = tagc[...]
    line = wide[...]
    middle, low = pltpu.roll(line, HD - ROWS, 1), pltpu.roll(line, HD - 2 * ROWS, 1)
    lse = jnp.where(tags >= 0.0, line + middle + low, masked_score)
    for s in range(slots):
        mine_s = jnp.where(tags == float(s), lse, masked_score)
        top_s[pl.ds(s, 1), :] = jnp.max(mine_s, axis=0, keepdims=True)
    top = jnp.maximum(top_s[...], new_peak)
    top_s[...] = top
    lane_top = jnp.zeros((peers, HD), F32)
    for s in range(slots):
        lane_top = jnp.where(tags == float(s), top_s[pl.ds(s, 1), :], lane_top)
    weight = jnp.exp(lse - lane_top)
    for s in range(slots):
        mine_s = jnp.where(tags == float(s), weight, 0.0)
        den_s[pl.ds(s, 1), :] = jnp.sum(mine_s, axis=0, keepdims=True)
    new_weight = jnp.exp(new_peak - top)
    inverse = 1.0 / (den_s[...] + new_total * new_weight)
    den_s[...] = inverse
    lane_inv = jnp.zeros((peers, HD), F32)
    for s in range(slots):
        lane_inv = jnp.where(tags == float(s), den_s[pl.ds(s, 1), :], lane_inv)
    wide[...] = weight * lane_inv
    new_share = new_weight * inverse

    on_row = iota((ROWS, HD), 0) == iota((ROWS, HD), 1)

    def weigh(l, carry):
        row = jnp.where(on_row, wide[pl.ds(l, 1), :], 0.0)
        column = jnp.sum(row, axis=1, keepdims=True)
        at = pl.ds(pl.multiple_of(l * ROWS, ROWS), ROWS)
        weighted[at, :] = (p_recv[l].astype(F32) * column).astype(BF16)
        return carry

    lax.fori_loop(0, peers, weigh, 0, unroll=8)
    mixed = jnp.dot(sel_t[...], weighted[...], preferred_element_type=F32)
    for r in range(rows):
        t, g = r // group, r % group
        at = slice(r * slots, (r + 1) * slots)
        res = mixed[at] + new_share[:, r : r + 1] * new_mixed[at, :]
        out_ref[t, :, g * HD : (g + 1) * HD] = res.astype(BF16)

    @pl.when(is_inner)
    def _():
        wait_for(low_recv.at[pl.ds(0, n_inner - 1)], low_send_sem.at[0])
        wait_for(low_total, low_send_sem.at[1])

    @pl.when(is_outer)
    def _():
        wait_for(low_recv.at[pl.ds(0, n_inner)], low_send_sem.at[0])

    wait_lanes(tag_recv, send_sem.at[0])
    wait_lanes(q_recv, send_sem.at[1])
    wait_lanes(p_recv, send_sem.at[2])


def on_device(
    x_rows,
    query_base_rows,
    k_base,
    value_base_rows,
    k_pool,
    v_pool,
    block_dest,
    block_slot,
    block_fill,
    a_query,
    query_up_factor,
    a_value,
    value_up_factor,
):
    peers, ranks = lax.axis_size("roll"), lax.axis_size("learn")
    steps, slots, width = x_rows.shape
    pool, block_len, _ = k_pool.shape
    rank = a_query.shape[1]
    a_query, a_value, block_dest = a_query.T, a_value.T, block_dest.T
    group = query_base_rows.shape[2] // HD
    chunk = width // ranks
    dims = (steps, slots, chunk, pool, block_len, group)
    hbm = pl.BlockSpec(memory_space=pltpu.HBM)
    smem = pl.BlockSpec(memory_space=pltpu.SMEM)
    vmem = pltpu.VMEM
    dma = pltpu.SemaphoreType.DMA
    return pl.pallas_call(
        functools.partial(kernel, peers, ranks, dims),
        out_shape=jax.ShapeDtypeStruct(query_base_rows.shape, BF16),
        in_specs=[hbm] * 6 + [smem] * 3 + [hbm] * 4,
        out_specs=pl.BlockSpec(memory_space=pltpu.VMEM),
        scratch_shapes=[
            vmem((steps, slots, chunk), BF16),
            vmem(query_base_rows.shape, BF16),
            vmem(k_base.shape, BF16),
            vmem(value_base_rows.shape, BF16),
            vmem(k_pool.shape, BF16),
            vmem(v_pool.shape, BF16),
            vmem((2 * rank, chunk), BF16),
            vmem(query_up_factor.shape, BF16),
            vmem(value_up_factor.shape, BF16),
            vmem((1, HD), F32),
            vmem((peers, HD), F32),
            vmem((1, HD), jnp.int32),
            pltpu.SMEM((1, HD), jnp.int32),
            vmem((ranks, steps * slots, 2 * rank), BF16),
            vmem((steps * slots, 2 * rank), BF16),
            vmem((peers, HD), F32),
            vmem((peers * ROWS, ROWS * slots), BF16),
            vmem((ROWS * slots, peers * ROWS), BF16),
            vmem((peers, ROWS, HD), BF16),
            vmem((peers, ROWS, HD), BF16),
            vmem((pool, ROWS, HD), BF16),
            vmem((peers, ROWS, HD), BF16),
            vmem((peers, ROWS, HD), BF16),
            vmem((ROWS * slots, HD), F32),
            vmem((slots, HD), F32),
            vmem((slots, HD), F32),
            vmem((peers, HD), F32),
            vmem((peers * ROWS, HD), BF16),
            dma((10,)),
            dma,
            dma((3,)),
            dma((3,)),
            dma((2,)),
            dma((2,)),
            pltpu.SemaphoreType.REGULAR,
            pltpu.SemaphoreType.REGULAR,
        ],
        compiler_params=pltpu.CompilerParams(
            collective_id=0, has_side_effects=True, vmem_limit_bytes=64 * 1024 * 1024
        ),
    )(
        x_rows,
        query_base_rows,
        k_base,
        value_base_rows,
        k_pool,
        v_pool,
        block_dest,
        block_slot,
        block_fill,
        a_query,
        query_up_factor,
        a_value,
        value_up_factor,
    )


def solution(mesh):
    return jax.shard_map(
        on_device,
        mesh=mesh,
        in_specs=(
            P(None, "roll", None),
            P(None, "roll", "learn"),
            P(None, "roll", "learn"),
            P(None, "roll", "learn"),
            P("roll", None, "learn"),
            P("roll", None, "learn"),
            P("roll", None),
            P("roll"),
            P("roll"),
            P("learn", None),
            P(None, "learn"),
            P("learn", None),
            P(None, "learn"),
        ),
        out_specs=P(None, "roll", "learn"),
        check_vma=False,
    )
```

```python
import functools
import math

import jax
import jax.numpy as jnp
from jax import lax
from jax.experimental import pallas as pl
from jax.experimental.pallas import tpu as pltpu
from jax.sharding import PartitionSpec as P

MESH = pl.DeviceIdType.MESH
F32 = jnp.float32
BF16 = jnp.bfloat16
HD = 128
ROWS = 16
adapter_scale = 0.5
masked_score = -1e30
no_slot = -1000.0


def iota(shape, dim):
    return lax.broadcasted_iota(jnp.int32, shape, dim)


def in_spare_row(column, tiles):
    n = column.shape[0]
    row, lane = lax.rem(iota((n, HD), 0), ROWS), iota((n, HD), 1)
    high = column.astype(BF16).astype(F32)
    middle = (column - high).astype(BF16).astype(F32)
    low = column - high - middle
    spread = jnp.where(lane == row, high, 0.0)
    spread = jnp.where(lane == row + ROWS, middle, spread)
    spread = jnp.where(lane == row + 2 * ROWS, low, spread)
    line = jnp.sum(spread.reshape(n // ROWS, ROWS, HD), axis=1, keepdims=True)
    tiles = tiles.reshape(n // ROWS, ROWS, HD)
    return jnp.where(iota(tiles.shape, 1) == ROWS - 1, line, tiles)


def kernel(
    peers,
    ranks,
    dims,
    x_hbm,
    qb_hbm,
    kb_hbm,
    vb_hbm,
    kp_hbm,
    vp_hbm,
    dest_hbm,
    slot_hbm,
    fill_hbm,
    aq_hbm,
    qu_hbm,
    av_hbm,
    vu_hbm,
    out_ref,
    x,
    dest,
    slot,
    fill,
    qb,
    kb,
    vb,
    kp,
    vp,
    a_both,
    qu,
    vu,
    tag_send,
    tag_recv,
    lane_vec,
    lane_blk,
    low_recv,
    low_total,
    tagc,
    sel,
    sel_t,
    q_send,
    q_recv,
    p_send,
    p_recv,
    new_mixed,
    top_s,
    den_s,
    wide,
    weighted,
    local_sem,
    blk_sem,
    send_sem,
    recv_sem,
    group_sem,
    low_send_sem,
    low_recv_sem,
    inner_in,
    roll_in,
):
    steps, slots, chunk, pool, block_len, group = dims
    rows = steps * group
    rank = aq_hbm.shape[0]
    me, ml = lax.axis_index("roll"), lax.axis_index("learn")
    others = pl.ds(0, peers - 1)

    chips = ranks // 2
    chip, core = ml // 2, lax.rem(ml, 2)
    partner = ml + 1 - 2 * core
    is_inner, is_outer = chip < 2, chip >= 2
    is_outer0 = jnp.logical_and(is_outer, core == 0)
    is_outer1 = jnp.logical_and(is_outer, core == 1)
    n_inner = 4
    barrier = pltpu.get_barrier_semaphore()
    gatherer = ml - core * (chip // 2)

    start = pl.multiple_of(ml * chunk, HD)
    pairs = [
        (x_hbm.at[:, :, pl.ds(start, chunk)], x),
        (aq_hbm, a_both.at[pl.ds(0, rank)]),
        (av_hbm, a_both.at[pl.ds(rank, rank)]),
        (qb_hbm, qb),
        (qu_hbm, qu),
        (kb_hbm, kb),
        (vb_hbm, vb),
        (vu_hbm, vu),
        (kp_hbm, kp),
        (vp_hbm, vp),
        (dest_hbm, dest),
        (slot_hbm, slot),
        (fill_hbm, fill),
    ]
    loads = [pltpu.make_async_copy(a, b, local_sem.at[i]) for i, (a, b) in enumerate(pairs)]
    for load in loads[:3]:
        load.start()

    def signal(sem, roll, learn):
        pl.semaphore_signal(sem, inc=1, device_id=(roll, learn), device_id_type=MESH)

    def greet(i, carry):
        signal(barrier, lax.rem(me + i, peers), gatherer)
        return carry

    signal(barrier, me, partner)

    @pl.when(is_inner)
    def _():
        signal(barrier, me, 2 - 2 * chip)
        signal(barrier, me, 3 - 2 * chip)
        for j in range(2, chips):
            signal(barrier, me, 2 * j + 1)

    @pl.when(is_inner)
    def _():
        lax.fori_loop(1, peers, greet, 0, unroll=7)

    for load in loads[3:]:
        load.start()

    for load in loads[:3]:
        load.wait()
    partial = lax.dot_general(
        x[...].reshape(steps * slots, chunk),
        a_both[...],
        (((1,), (1,)), ((), ())),
        preferred_element_type=F32,
    )
    low_recv[ml] = partial.astype(BF16)

    def to_learn(src, dst, k, learn):
        return pltpu.make_async_remote_copy(
            src_ref=src,
            dst_ref=dst,
            send_sem=low_send_sem.at[k],
            recv_sem=low_recv_sem.at[k],
            device_id=(me, learn),
            device_id_type=MESH,
        )

    @pl.when(is_inner)
    def _():
        pl.semaphore_wait(barrier, peers + 2)

    @pl.when(is_outer1)
    def _():
        pl.semaphore_wait(barrier, n_inner + 1)
        signal(inner_in, me, partner)

    @pl.when(is_outer0)
    def _():
        pl.semaphore_wait(inner_in, 1)

    my_low = low_recv.at[ml]

    @pl.when(is_inner)
    def _():
        to_learn(my_low, my_low, 0, partner).start()
        to_learn(my_low, my_low, 0, 2 - 2 * chip).start()
        to_learn(my_low, my_low, 0, 3 - 2 * chip).start()

    @pl.when(is_outer)
    def _():
        for j in range(n_inner):
            to_learn(my_low, my_low, 0, j).start()

    @pl.when(is_outer)
    def _():
        lax.fori_loop(1, peers, greet, 0, unroll=7)

    for load in loads[10:12]:
        load.wait()
    lane = iota((1, HD), 1)
    tag_row = jnp.full((1, HD), no_slot, F32)
    blk_row = jnp.zeros((1, HD), jnp.int32)
    for b in range(pool):
        hit = lane == dest[0, b]
        tag_row = jnp.where(hit, slot[b].astype(F32), tag_row)
        blk_row = jnp.where(hit, b, blk_row)
    tag_send[...] = tag_row
    tag_recv[pl.ds(me, 1), :] = tag_row
    lane_vec[...] = blk_row
    to_smem = pltpu.make_async_copy(lane_vec, lane_blk, blk_sem)
    to_smem.start()

    @pl.when(is_outer0)
    def _():
        pl.semaphore_wait(barrier, 2 * peers - 1)
        signal(roll_in, me, partner)

    @pl.when(is_outer1)
    def _():
        pl.semaphore_wait(roll_in, 1)

    def to_roll(src_of, dst, k):
        def one(i, carry):
            d = lax.rem(me + i, peers)
            pltpu.make_async_remote_copy(
                src_ref=src_of(d),
                dst_ref=dst,
                send_sem=send_sem.at[k],
                recv_sem=recv_sem.at[k],
                device_id=(d, ml),
                device_id_type=MESH,
            ).start()
            return carry

        lax.fori_loop(1, peers, one, 0)

    side = 4
    plane = side * side
    my_y, my_z, my_x = me // plane, lax.rem(me // side, side), lax.rem(me, side)
    z_of = [my_z, my_z + 1 - 2 * lax.rem(my_z, 2), lax.rem(my_z + 2, side), side - 1 - my_z]

    def lane_at(c, i):
        over = lax.rem(2 * (i // side), side) + i // (2 * side)
        return (
            lax.rem(my_y + over, side) * plane
            + z_of[c] * side
            + lax.rem(my_x + lax.rem(i, side), side)
        )

    batch = 8
    groups = [(c, f) for c in range(side) for f in range(0, plane, batch)]

    def lanes_of(group):
        c, f = group
        return [lane_at(c, f + j) for j in range(batch)]

    def to_group(group, src, dst, k):
        c, f = group
        n = (c * plane + f) // batch

        def one(j, carry):
            d = lane_at(c, f + j)
            pltpu.make_async_remote_copy(
                src_ref=src.at[n * batch + j],
                dst_ref=dst.at[me],
                send_sem=send_sem.at[k],
                recv_sem=group_sem.at[k - 1, n],
                device_id=(d, ml),
                device_id_type=MESH,
            ).start()
            return carry

        lax.fori_loop(int(n == 0), batch, one, 0)

    def wait_group(group, buf, k):
        c, f = group
        n = (c * plane + f) // batch
        wait_for(buf.at[pl.ds(0, batch - int(n == 0))], group_sem.at[k - 1, n])

    to_roll(lambda d: tag_send, tag_recv.at[pl.ds(me, 1), :], 0)


    def wait_lanes(buf, sem):
        pltpu.make_async_copy(buf.at[others], buf.at[others], sem).wait()

    def wait_for(ref, sem):
        pltpu.make_async_copy(ref, ref, sem).wait()

    wait_lanes(tag_recv, recv_sem.at[0])
    mine = iota((peers, HD), 1) == me
    asked = jnp.sum(jnp.where(mine, tag_recv[...], 0.0), axis=1, keepdims=True)
    tagc[...] = jnp.broadcast_to(asked, (peers, HD))

    width = ROWS * slots
    sel_row = (iota((ROWS, width), 0) * slots).astype(F32)
    sel_lane = iota((ROWS, width), 1).astype(F32)

    def pick(c, i, carry):
        row = tagc[pl.ds(lane_at(c, i), 1), :]
        want = sel_row + jnp.concatenate([row] * (width // HD), axis=1)
        hot = jnp.where(want == sel_lane, 1.0, 0.0).astype(BF16)
        sel[pl.ds(pl.multiple_of((c * plane + i) * ROWS, ROWS), ROWS), :] = hot
        return carry

    for c in range(side):
        lax.fori_loop(0, plane, functools.partial(pick, c), 0, unroll=8)

    for load in loads[3:5]:
        load.wait()

    @pl.when(is_inner)
    def _():
        wait_for(low_recv.at[pl.ds(0, ranks - 1)], low_recv_sem.at[0])
        summed = functools.reduce(jnp.add, [low_recv[j].astype(F32) for j in range(ranks)])
        low_total[...] = summed.astype(BF16)
        to_learn(low_total, low_total, 1, 2 * (chips - 1 - chip) + core).start()

    @pl.when(is_outer)
    def _():
        wait_for(low_total, low_recv_sem.at[1])

    up = jnp.dot(low_total[:, :rank], qu[...], preferred_element_type=F32)
    query = qb[...].reshape(steps * slots, group * HD).astype(F32) + adapter_scale * up
    query = query.astype(BF16)
    tiles = [
        query[t * slots : (t + 1) * slots, g * HD : (g + 1) * HD]
        for t in range(steps)
        for g in range(group)
    ]
    stack = jnp.concatenate(tiles + [jnp.zeros((slots, HD), BF16)] * (ROWS - rows), axis=0)
    for c in range(side):
        mine = pl.ds(c * plane * ROWS, plane * ROWS)
        picked = jnp.dot(sel[mine, :], stack, preferred_element_type=F32).astype(BF16)
        q_send[pl.ds(c * plane, plane)] = picked.reshape(plane, ROWS, HD)
        for f in range(0, plane, batch):
            to_group((c, f), q_send, q_recv, 1)
    q_recv[me] = q_send[0]

    sel_t[...] = sel[...].T

    for load in loads[8:10] + loads[12:]:
        load.wait()
    to_smem.wait()
    scale = 1.0 / math.sqrt(HD)
    token = iota((ROWS, block_len), 1)

    def some_lanes(group):
        lanes = lanes_of(group)
        first = group[0] * plane + group[1]
        blocks = [lane_blk[0, d] for d in lanes]
        scored = []
        for j in range(0, batch, 2):
            queries = jnp.concatenate([q_recv[d] for d in lanes[j : j + 2]], axis=0)
            keys = jnp.concatenate([kp[b] for b in blocks[j : j + 2]], axis=0)
            s = lax.dot_general(
                queries, keys, (((1,), (1,)), ((), ())), preferred_element_type=F32
            )
            for h in range(2):
                own = s[h * ROWS : (h + 1) * ROWS, h * block_len : (h + 1) * block_len]
                scored.append(jnp.where(token < fill[blocks[j + h]], own * scale, masked_score))
        s = jnp.concatenate(scored, axis=0)
        peak = jnp.max(s, axis=1, keepdims=True)
        w = jnp.exp(s - peak)
        total = jnp.sum(w, axis=1, keepdims=True)
        w16 = w.astype(BF16)
        mixed = []
        for j in range(0, batch, 2):
            values = jnp.concatenate([vp[b] for b in blocks[j : j + 2]], axis=1)
            m = jnp.dot(w16[j * ROWS : (j + 2) * ROWS], values, preferred_element_type=F32)
            mixed += [m[:ROWS, :HD], m[ROWS:, HD:]]
        mixed = jnp.concatenate(mixed, axis=0)
        tiles = in_spare_row(peak + jnp.log(total), mixed / total).astype(BF16)
        p_send[pl.ds(first, batch)] = tiles

    for lanes_group in groups:
        wait_group(lanes_group, q_recv, 1)
        some_lanes(lanes_group)
        to_group(lanes_group, p_send, p_recv, 2)
    p_recv[me] = p_send[0]

    for load in loads[5:8]:
        load.wait()
    up_v = jnp.dot(low_total[:, rank:], vu[...], preferred_element_type=F32)
    value = vb[...].reshape(steps * slots, HD).astype(F32) + adapter_scale * up_v
    value = value.astype(BF16).astype(F32)
    values = [value[t * slots : (t + 1) * slots] for t in range(steps)]
    keys = [kb[t].astype(F32) for t in range(steps)]
    lane_s = iota((slots, HD), 1)
    scores = [jnp.full((slots, HD), masked_score, F32) for _ in range(steps)]
    for r in range(rows):
        q_r = tiles[r].astype(F32)
        for u in range(r // group + 1):
            s = jnp.sum(q_r * keys[u], axis=1, keepdims=True) * scale
            scores[u] = jnp.where(lane_s == r, s, scores[u])
    new_peak = functools.reduce(jnp.maximum, scores)
    new_w = [
        jnp.where(lane_s >= u * group, jnp.exp(scores[u] - new_peak), 0.0) for u in range(steps)
    ]
    new_total = functools.reduce(jnp.add, new_w)
    rounded = [w.astype(BF16).astype(F32) for w in new_w]
    for r in range(rows):
        acc = jnp.zeros((slots, HD), F32)
        for u in range(r // group + 1):
            acc = acc + rounded[u][:, r : r + 1] * values[u]
        new_mixed[pl.ds(r * slots, slots), :] = acc

    def spare_row(c, i, carry):
        d = lane_at(c, i)
        wide[pl.ds(d, 1), :] = p_recv[d].astype(F32)[ROWS - 1 :]
        return carry

    for c, f in groups:
        wait_group((c, f), p_recv, 2)
        for i in range(f, f + batch):
            spare_row(c, i, 0)
    tags = tagc[...]
    line = wide[...]
    middle, low = pltpu.roll(line, HD - ROWS, 1), pltpu.roll(line, HD - 2 * ROWS, 1)
    lse = jnp.where(tags >= 0.0, line + middle + low, masked_score)
    for s in range(slots):
        mine_s = jnp.where(tags == float(s), lse, masked_score)
        top_s[pl.ds(s, 1), :] = jnp.max(mine_s, axis=0, keepdims=True)
    top = jnp.maximum(top_s[...], new_peak)
    top_s[...] = top
    lane_top = jnp.zeros((peers, HD), F32)
    for s in range(slots):
        lane_top = jnp.where(tags == float(s), top_s[pl.ds(s, 1), :], lane_top)
    weight = jnp.exp(lse - lane_top)
    for s in range(slots):
        mine_s = jnp.where(tags == float(s), weight, 0.0)
        den_s[pl.ds(s, 1), :] = jnp.sum(mine_s, axis=0, keepdims=True)
    new_weight = jnp.exp(new_peak - top)
    inverse = 1.0 / (den_s[...] + new_total * new_weight)
    wide[...] = weight
    on_row = iota((ROWS, HD), 0) == iota((ROWS, HD), 1)

    def weigh(c, i, carry):
        d = lane_at(c, i)
        row = jnp.where(on_row, wide[pl.ds(d, 1), :], 0.0)
        column = jnp.sum(row, axis=1, keepdims=True)
        at = pl.ds(pl.multiple_of((c * plane + i) * ROWS, ROWS), ROWS)
        weighted[at, :] = (p_recv[d].astype(F32) * column).astype(BF16)
        return carry

    for c in range(side):
        lax.fori_loop(0, plane, functools.partial(weigh, c), 0, unroll=16)
    mixed = jnp.dot(sel_t[...], weighted[...], preferred_element_type=F32)
    for r in range(rows):
        t, g = r // group, r % group
        at = slice(r * slots, (r + 1) * slots)
        res = mixed[at] + new_weight[:, r : r + 1] * new_mixed[at, :]
        res = res * inverse[:, r : r + 1]
        out_ref[t, :, g * HD : (g + 1) * HD] = res.astype(BF16)

    @pl.when(is_inner)
    def _():
        wait_for(low_recv.at[pl.ds(0, n_inner - 1)], low_send_sem.at[0])
        wait_for(low_total, low_send_sem.at[1])

    @pl.when(is_outer)
    def _():
        wait_for(low_recv.at[pl.ds(0, n_inner)], low_send_sem.at[0])

    wait_lanes(tag_recv, send_sem.at[0])
    wait_lanes(q_recv, send_sem.at[1])
    wait_lanes(p_recv, send_sem.at[2])


def on_device(
    x_rows,
    query_base_rows,
    k_base,
    value_base_rows,
    k_pool,
    v_pool,
    block_dest,
    block_slot,
    block_fill,
    a_query,
    query_up_factor,
    a_value,
    value_up_factor,
):
    peers, ranks = lax.axis_size("roll"), lax.axis_size("learn")
    steps, slots, width = x_rows.shape
    pool, block_len, _ = k_pool.shape
    rank = a_query.shape[1]
    a_query, a_value, block_dest = a_query.T, a_value.T, block_dest.T
    group = query_base_rows.shape[2] // HD
    chunk = width // ranks
    dims = (steps, slots, chunk, pool, block_len, group)
    hbm = pl.BlockSpec(memory_space=pltpu.HBM)
    vmem = pltpu.VMEM
    dma = pltpu.SemaphoreType.DMA
    return pl.pallas_call(
        functools.partial(kernel, peers, ranks, dims),
        out_shape=jax.ShapeDtypeStruct(query_base_rows.shape, BF16),
        in_specs=[hbm] * 13,
        out_specs=pl.BlockSpec(memory_space=pltpu.VMEM),
        scratch_shapes=[
            vmem((steps, slots, chunk), BF16),
            pltpu.SMEM(block_dest.shape, jnp.int32),
            pltpu.SMEM(block_slot.shape, jnp.int32),
            pltpu.SMEM(block_fill.shape, jnp.int32),
            vmem(query_base_rows.shape, BF16),
            vmem(k_base.shape, BF16),
            vmem(value_base_rows.shape, BF16),
            vmem(k_pool.shape, BF16),
            vmem(v_pool.shape, BF16),
            vmem((2 * rank, chunk), BF16),
            vmem(query_up_factor.shape, BF16),
            vmem(value_up_factor.shape, BF16),
            vmem((1, HD), F32),
            vmem((peers, HD), F32),
            vmem((1, HD), jnp.int32),
            pltpu.SMEM((1, HD), jnp.int32),
            vmem((ranks, steps * slots, 2 * rank), BF16),
            vmem((steps * slots, 2 * rank), BF16),
            vmem((peers, HD), F32),
            vmem((peers * ROWS, ROWS * slots), BF16),
            vmem((ROWS * slots, peers * ROWS), BF16),
            vmem((peers, ROWS, HD), BF16),
            vmem((peers, ROWS, HD), BF16),
            vmem((peers, ROWS, HD), BF16),
            vmem((peers, ROWS, HD), BF16),
            vmem((ROWS * slots, HD), F32),
            vmem((slots, HD), F32),
            vmem((slots, HD), F32),
            vmem((peers, HD), F32),
            vmem((peers * ROWS, HD), BF16),
            dma((13,)),
            dma,
            dma((3,)),
            dma((1,)),
            dma((2, 8)),
            dma((2,)),
            dma((2,)),
            pltpu.SemaphoreType.REGULAR,
            pltpu.SemaphoreType.REGULAR,
        ],
        compiler_params=pltpu.CompilerParams(
            collective_id=0, has_side_effects=True, vmem_limit_bytes=64 * 1024 * 1024
        ),
    )(
        x_rows,
        query_base_rows,
        k_base,
        value_base_rows,
        k_pool,
        v_pool,
        block_dest,
        block_slot,
        block_fill,
        a_query,
        query_up_factor,
        a_value,
        value_up_factor,
    )


def solution(mesh):
    return jax.shard_map(
        on_device,
        mesh=mesh,
        in_specs=(
            P(None, "roll", None),
            P(None, "roll", "learn"),
            P(None, "roll", "learn"),
            P(None, "roll", "learn"),
            P("roll", None, "learn"),
            P("roll", None, "learn"),
            P("roll", None),
            P("roll"),
            P("roll"),
            P("learn", None),
            P(None, "learn"),
            P("learn", None),
            P(None, "learn"),
        ),
        out_specs=P(None, "roll", "learn"),
        check_vma=False,
    )
```

```python
import functools
import math

import jax
import jax.numpy as jnp
from jax import lax
from jax.experimental import pallas as pl
from jax.experimental.pallas import tpu as pltpu
from jax.sharding import PartitionSpec as P

MESH = pl.DeviceIdType.MESH
F32 = jnp.float32
BF16 = jnp.bfloat16
HD = 128
ROWS = 16
adapter_scale = 0.5
masked_score = -1e30
no_slot = -1000.0


def iota(shape, dim):
    return lax.broadcasted_iota(jnp.int32, shape, dim)


def in_spare_row(column, tiles):
    n = column.shape[0]
    row, lane = lax.rem(iota((n, HD), 0), ROWS), iota((n, HD), 1)
    high = column.astype(BF16).astype(F32)
    middle = (column - high).astype(BF16).astype(F32)
    low = column - high - middle
    spread = jnp.where(lane == row, high, 0.0)
    spread = jnp.where(lane == row + ROWS, middle, spread)
    spread = jnp.where(lane == row + 2 * ROWS, low, spread)
    line = jnp.sum(spread.reshape(n // ROWS, ROWS, HD), axis=1, keepdims=True)
    tiles = tiles.reshape(n // ROWS, ROWS, HD)
    return jnp.where(iota(tiles.shape, 1) == ROWS - 1, line, tiles)


def kernel(
    peers,
    ranks,
    dims,
    x_hbm,
    qb_hbm,
    kb_hbm,
    vb_hbm,
    kp_hbm,
    vp_hbm,
    dest_hbm,
    slot_hbm,
    fill_hbm,
    aq_hbm,
    qu_hbm,
    av_hbm,
    vu_hbm,
    out_ref,
    x,
    dest,
    slot,
    fill,
    qb,
    kb,
    vb,
    kp,
    vp,
    a_both,
    qu,
    vu,
    tag_send,
    tag_recv,
    lane_vec,
    lane_blk,
    low_recv,
    low_total,
    tagc,
    sel,
    sel_t,
    q_send,
    q_recv,
    p_send,
    p_recv,
    new_mixed,
    top_s,
    den_s,
    wide,
    weighted,
    local_sem,
    blk_sem,
    send_sem,
    recv_sem,
    group_sem,
    low_send_sem,
    low_recv_sem,
    inner_in,
    roll_in,
):
    steps, slots, chunk, pool, block_len, group = dims
    rows = steps * group
    rank = aq_hbm.shape[0]
    me, ml = lax.axis_index("roll"), lax.axis_index("learn")
    others = pl.ds(0, peers - 1)

    chips = ranks // 2
    chip, core = ml // 2, lax.rem(ml, 2)
    partner = ml + 1 - 2 * core
    is_inner, is_outer = chip == 0, chip > 0
    is_outer0 = jnp.logical_and(is_outer, core == 0)
    is_outer1 = jnp.logical_and(is_outer, core == 1)
    n_inner = 2
    barrier = pltpu.get_barrier_semaphore()
    gatherer = ml - core * ((chip + chips - 1) // chips)

    start = pl.multiple_of(ml * chunk, HD)
    pairs = [
        (x_hbm.at[:, :, pl.ds(start, chunk)], x),
        (aq_hbm, a_both.at[pl.ds(0, rank)]),
        (av_hbm, a_both.at[pl.ds(rank, rank)]),
        (qb_hbm, qb),
        (qu_hbm, qu),
        (kb_hbm, kb),
        (vb_hbm, vb),
        (vu_hbm, vu),
        (kp_hbm, kp),
        (vp_hbm, vp),
        (dest_hbm, dest),
        (slot_hbm, slot),
        (fill_hbm, fill),
    ]
    loads = [pltpu.make_async_copy(a, b, local_sem.at[i]) for i, (a, b) in enumerate(pairs)]
    for load in loads[:3]:
        load.start()

    def signal(sem, roll, learn):
        pl.semaphore_signal(sem, inc=1, device_id=(roll, learn), device_id_type=MESH)

    def greet(i, carry):
        signal(barrier, lax.rem(me + i, peers), gatherer)
        return carry

    signal(barrier, me, partner)

    @pl.when(is_inner)
    def _():
        for j in range(1, chips):
            signal(barrier, me, 2 * j + 1)

    @pl.when(is_inner)
    def _():
        lax.fori_loop(1, peers, greet, 0, unroll=7)

    for load in loads[3:]:
        load.start()

    half = steps * slots // 2
    urgent = 2 * ROWS

    def packed(low):
        return jnp.concatenate([low[:half], low[half:]], axis=1)

    def unpacked(low):
        return jnp.concatenate([low[:, :rank], low[:, rank:]], axis=0).astype(BF16)

    def make_partial():
        for load in loads[:3]:
            load.wait()
        partial = lax.dot_general(
            x[...].reshape(steps * slots, chunk),
            a_both[...],
            (((1,), (1,)), ((), ())),
            preferred_element_type=F32,
        )
        both = jnp.concatenate([packed(partial[:, :rank]), packed(partial[:, rank:])], axis=0)
        low_recv[ml] = both.astype(BF16)

    def to_learn(src, dst, k, learn):
        return pltpu.make_async_remote_copy(
            src_ref=src,
            dst_ref=dst,
            send_sem=low_send_sem.at[k],
            recv_sem=low_recv_sem.at[k],
            device_id=(me, learn),
            device_id_type=MESH,
        )

    low_parts = [pl.ds(0, urgent), pl.ds(urgent, steps * slots - urgent)]

    def send_partial(k, targets):
        mine = low_recv.at[ml, low_parts[k]]
        for target in targets:
            to_learn(mine, mine, k, target).start()

    @pl.when(is_outer)
    def _():
        make_partial()

    @pl.when(is_outer1)
    def _():
        pl.semaphore_wait(barrier, n_inner + 1)
        signal(inner_in, me, partner)

    @pl.when(is_outer0)
    def _():
        pl.semaphore_wait(inner_in, 1)

    @pl.when(is_outer)
    def _():
        send_partial(0, range(n_inner))
        lax.fori_loop(1, peers, greet, 0, unroll=7)

    for load in loads[10:12]:
        load.wait()
    lane = iota((1, HD), 1)
    tag_row = jnp.full((1, HD), no_slot, F32)
    blk_row = jnp.zeros((1, HD), jnp.int32)
    for b in range(pool):
        hit = lane == dest[0, b]
        tag_row = jnp.where(hit, slot[b].astype(F32), tag_row)
        blk_row = jnp.where(hit, b, blk_row)
    tag_send[...] = tag_row
    tag_recv[pl.ds(me, 1), :] = tag_row
    lane_vec[...] = blk_row
    to_smem = pltpu.make_async_copy(lane_vec, lane_blk, blk_sem)
    to_smem.start()

    @pl.when(is_inner)
    def _():
        make_partial()
        pl.semaphore_wait(barrier, peers)

    @pl.when(is_outer0)
    def _():
        pl.semaphore_wait(barrier, 2 * peers - 1)
        signal(roll_in, me, partner)

    @pl.when(is_outer1)
    def _():
        pl.semaphore_wait(roll_in, 1)

    def to_roll(src_of, dst, k):
        def one(i, carry):
            d = lax.rem(me + i, peers)
            pltpu.make_async_remote_copy(
                src_ref=src_of(d),
                dst_ref=dst,
                send_sem=send_sem.at[k],
                recv_sem=recv_sem.at[k],
                device_id=(d, ml),
                device_id_type=MESH,
            ).start()
            return carry

        lax.fori_loop(1, peers, one, 0)

    side = 4
    plane = side * side
    my_y, my_z, my_x = me // plane, lax.rem(me // side, side), lax.rem(me, side)
    z_of = [my_z, my_z + 1 - 2 * lax.rem(my_z, 2), lax.rem(my_z + 2, side), side - 1 - my_z]

    def lane_at(c, i):
        over = lax.rem(2 * (i // side), side) + i // (2 * side)
        return (
            lax.rem(my_y + over, side) * plane
            + z_of[c] * side
            + lax.rem(my_x + lax.rem(i, side), side)
        )

    batch = 8
    groups = [(c, f) for c in range(side) for f in range(0, plane, batch)]

    def lanes_of(group):
        c, f = group
        return [lane_at(c, f + j) for j in range(batch)]

    def to_group(group, src, dst, k):
        c, f = group
        n = (c * plane + f) // batch

        def one(j, carry):
            d = lane_at(c, f + j)
            pltpu.make_async_remote_copy(
                src_ref=src.at[n * batch + j],
                dst_ref=dst.at[me],
                send_sem=send_sem.at[k],
                recv_sem=group_sem.at[k - 1, n],
                device_id=(d, ml),
                device_id_type=MESH,
            ).start()
            return carry

        lax.fori_loop(int(n == 0), batch, one, 0)

    def wait_group(group, buf, k):
        c, f = group
        n = (c * plane + f) // batch
        wait_for(buf.at[pl.ds(0, batch - int(n == 0))], group_sem.at[k - 1, n])

    to_roll(lambda d: tag_send, tag_recv.at[pl.ds(me, 1), :], 0)


    @pl.when(is_inner)
    def _():
        send_partial(0, [partner])
        send_partial(1, [partner])

    @pl.when(is_outer)
    def _():
        send_partial(1, range(n_inner))

    def wait_lanes(buf, sem):
        pltpu.make_async_copy(buf.at[others], buf.at[others], sem).wait()

    def wait_for(ref, sem):
        pltpu.make_async_copy(ref, ref, sem).wait()

    wait_lanes(tag_recv, recv_sem.at[0])
    mine = iota((peers, HD), 1) == me
    asked = jnp.sum(jnp.where(mine, tag_recv[...], 0.0), axis=1, keepdims=True)
    tagc[...] = jnp.broadcast_to(asked, (peers, HD))

    width = ROWS * slots
    sel_row = (iota((ROWS, width), 0) * slots).astype(F32)
    sel_lane = iota((ROWS, width), 1).astype(F32)

    def pick(c, i, carry):
        row = tagc[pl.ds(lane_at(c, i), 1), :]
        want = sel_row + jnp.concatenate([row] * (width // HD), axis=1)
        hot = jnp.where(want == sel_lane, 1.0, 0.0).astype(BF16)
        sel[pl.ds(pl.multiple_of((c * plane + i) * ROWS, ROWS), ROWS), :] = hot
        return carry

    for c in range(side):
        lax.fori_loop(0, plane, functools.partial(pick, c), 0, unroll=8)

    for load in loads[3:5]:
        load.wait()

    def sum_part(k):
        at = low_parts[k]

        @pl.when(is_inner)
        def _():
            wait_for(low_recv.at[pl.ds(0, ranks - 1), at], low_recv_sem.at[k])
            summed = functools.reduce(
                jnp.add, [low_recv[j, at, :].astype(F32) for j in range(ranks)]
            )
            low_total[at, :] = summed.astype(BF16)
            total = low_total.at[at]
            for j in range(1, chips):
                to_learn(total, total, k + 2, 2 * j + core).start()

        @pl.when(is_outer)
        def _():
            wait_for(low_total.at[at], low_recv_sem.at[k + 2])

    sum_part(0)
    low_q = unpacked(low_total[:urgent, :].astype(F32)[:half])
    up = jnp.dot(low_q, qu[...], preferred_element_type=F32)
    query = qb[...].reshape(steps * slots, group * HD).astype(F32) + adapter_scale * up
    query = query.astype(BF16)
    tiles = [
        query[t * slots : (t + 1) * slots, g * HD : (g + 1) * HD]
        for t in range(steps)
        for g in range(group)
    ]
    stack = jnp.concatenate(tiles + [jnp.zeros((slots, HD), BF16)] * (ROWS - rows), axis=0)
    for c in range(side):
        mine = pl.ds(c * plane * ROWS, plane * ROWS)
        picked = jnp.dot(sel[mine, :], stack, preferred_element_type=F32).astype(BF16)
        q_send[pl.ds(c * plane, plane)] = picked.reshape(plane, ROWS, HD)
        for f in range(0, plane, batch):
            to_group((c, f), q_send, q_recv, 1)
    q_recv[me] = q_send[0]

    sum_part(1)
    sel_t[...] = sel[...].T

    for load in loads[8:10] + loads[12:]:
        load.wait()
    to_smem.wait()
    scale = 1.0 / math.sqrt(HD)
    token = iota((ROWS, block_len), 1)

    def some_lanes(group):
        lanes = lanes_of(group)
        first = group[0] * plane + group[1]
        blocks = [lane_blk[0, d] for d in lanes]
        scored = []
        for j in range(0, batch, 2):
            queries = jnp.concatenate([q_recv[d] for d in lanes[j : j + 2]], axis=0)
            keys = jnp.concatenate([kp[b] for b in blocks[j : j + 2]], axis=0)
            s = lax.dot_general(
                queries, keys, (((1,), (1,)), ((), ())), preferred_element_type=F32
            )
            for h in range(2):
                own = s[h * ROWS : (h + 1) * ROWS, h * block_len : (h + 1) * block_len]
                scored.append(jnp.where(token < fill[blocks[j + h]], own * scale, masked_score))
        s = jnp.concatenate(scored, axis=0)
        peak = jnp.max(s, axis=1, keepdims=True)
        w = jnp.exp(s - peak)
        total = jnp.sum(w, axis=1, keepdims=True)
        w16 = w.astype(BF16)
        mixed = []
        for j in range(0, batch, 2):
            values = jnp.concatenate([vp[b] for b in blocks[j : j + 2]], axis=1)
            m = jnp.dot(w16[j * ROWS : (j + 2) * ROWS], values, preferred_element_type=F32)
            mixed += [m[:ROWS, :HD], m[ROWS:, HD:]]
        mixed = jnp.concatenate(mixed, axis=0)
        tiles = in_spare_row(peak + jnp.log(total), mixed / total).astype(BF16)
        p_send[pl.ds(first, batch)] = tiles

    for lanes_group in groups:
        wait_group(lanes_group, q_recv, 1)
        some_lanes(lanes_group)
        to_group(lanes_group, p_send, p_recv, 2)
    p_recv[me] = p_send[0]

    for load in loads[5:8]:
        load.wait()
    low_v = unpacked(low_total[...].astype(F32)[half:])
    up_v = jnp.dot(low_v, vu[...], preferred_element_type=F32)
    value = vb[...].reshape(steps * slots, HD).astype(F32) + adapter_scale * up_v
    value = value.astype(BF16).astype(F32)
    values = [value[t * slots : (t + 1) * slots] for t in range(steps)]
    keys = [kb[t].astype(F32) for t in range(steps)]
    lane_s = iota((slots, HD), 1)
    scores = [jnp.full((slots, HD), masked_score, F32) for _ in range(steps)]
    for r in range(rows):
        q_r = tiles[r].astype(F32)
        for u in range(r // group + 1):
            s = jnp.sum(q_r * keys[u], axis=1, keepdims=True) * scale
            scores[u] = jnp.where(lane_s == r, s, scores[u])
    new_peak = functools.reduce(jnp.maximum, scores)
    new_w = [
        jnp.where(lane_s >= u * group, jnp.exp(scores[u] - new_peak), 0.0) for u in range(steps)
    ]
    new_total = functools.reduce(jnp.add, new_w)
    rounded = [w.astype(BF16).astype(F32) for w in new_w]
    for r in range(rows):
        acc = jnp.zeros((slots, HD), F32)
        for u in range(r // group + 1):
            acc = acc + rounded[u][:, r : r + 1] * values[u]
        new_mixed[pl.ds(r * slots, slots), :] = acc

    def spare_row(c, i, carry):
        d = lane_at(c, i)
        wide[pl.ds(d, 1), :] = p_recv[d].astype(F32)[ROWS - 1 :]
        return carry

    for c, f in groups:
        wait_group((c, f), p_recv, 2)
        for i in range(f, f + batch):
            spare_row(c, i, 0)
    tags = tagc[...]
    line = wide[...]
    middle, low = pltpu.roll(line, HD - ROWS, 1), pltpu.roll(line, HD - 2 * ROWS, 1)
    lse = jnp.where(tags >= 0.0, line + middle + low, masked_score)
    for s in range(slots):
        mine_s = jnp.where(tags == float(s), lse, masked_score)
        top_s[pl.ds(s, 1), :] = jnp.max(mine_s, axis=0, keepdims=True)
    top = jnp.maximum(top_s[...], new_peak)
    top_s[...] = top
    lane_top = jnp.zeros((peers, HD), F32)
    for s in range(slots):
        lane_top = jnp.where(tags == float(s), top_s[pl.ds(s, 1), :], lane_top)
    weight = jnp.exp(lse - lane_top)
    for s in range(slots):
        mine_s = jnp.where(tags == float(s), weight, 0.0)
        den_s[pl.ds(s, 1), :] = jnp.sum(mine_s, axis=0, keepdims=True)
    new_weight = jnp.exp(new_peak - top)
    inverse = 1.0 / (den_s[...] + new_total * new_weight)
    wide[...] = weight
    on_row = iota((ROWS, HD), 0) == iota((ROWS, HD), 1)

    def weigh(c, i, carry):
        d = lane_at(c, i)
        row = jnp.where(on_row, wide[pl.ds(d, 1), :], 0.0)
        column = jnp.sum(row, axis=1, keepdims=True)
        at = pl.ds(pl.multiple_of((c * plane + i) * ROWS, ROWS), ROWS)
        weighted[at, :] = (p_recv[d].astype(F32) * column).astype(BF16)
        return carry

    for c in range(side):
        lax.fori_loop(0, plane, functools.partial(weigh, c), 0, unroll=16)
    mixed = jnp.dot(sel_t[...], weighted[...], preferred_element_type=F32)
    for r in range(rows):
        t, g = r // group, r % group
        at = slice(r * slots, (r + 1) * slots)
        res = mixed[at] + new_weight[:, r : r + 1] * new_mixed[at, :]
        res = res * inverse[:, r : r + 1]
        out_ref[t, :, g * HD : (g + 1) * HD] = res.astype(BF16)

    @pl.when(is_inner)
    def _():
        for k in range(2):
            wait_for(low_recv.at[0, low_parts[k]], low_send_sem.at[k])
            wait_for(low_recv.at[pl.ds(0, chips - 1), low_parts[k]], low_send_sem.at[k + 2])

    @pl.when(is_outer)
    def _():
        for k in range(2):
            wait_for(low_recv.at[pl.ds(0, n_inner), low_parts[k]], low_send_sem.at[k])

    wait_lanes(tag_recv, send_sem.at[0])
    wait_lanes(q_recv, send_sem.at[1])
    wait_lanes(p_recv, send_sem.at[2])


def on_device(
    x_rows,
    query_base_rows,
    k_base,
    value_base_rows,
    k_pool,
    v_pool,
    block_dest,
    block_slot,
    block_fill,
    a_query,
    query_up_factor,
    a_value,
    value_up_factor,
):
    peers, ranks = lax.axis_size("roll"), lax.axis_size("learn")
    steps, slots, width = x_rows.shape
    pool, block_len, _ = k_pool.shape
    rank = a_query.shape[1]
    a_query, a_value, block_dest = a_query.T, a_value.T, block_dest.T
    group = query_base_rows.shape[2] // HD
    chunk = width // ranks
    dims = (steps, slots, chunk, pool, block_len, group)
    hbm = pl.BlockSpec(memory_space=pltpu.HBM)
    vmem = pltpu.VMEM
    dma = pltpu.SemaphoreType.DMA
    return pl.pallas_call(
        functools.partial(kernel, peers, ranks, dims),
        out_shape=jax.ShapeDtypeStruct(query_base_rows.shape, BF16),
        in_specs=[hbm] * 13,
        out_specs=pl.BlockSpec(memory_space=pltpu.VMEM),
        scratch_shapes=[
            vmem((steps, slots, chunk), BF16),
            pltpu.SMEM(block_dest.shape, jnp.int32),
            pltpu.SMEM(block_slot.shape, jnp.int32),
            pltpu.SMEM(block_fill.shape, jnp.int32),
            vmem(query_base_rows.shape, BF16),
            vmem(k_base.shape, BF16),
            vmem(value_base_rows.shape, BF16),
            vmem(k_pool.shape, BF16),
            vmem(v_pool.shape, BF16),
            vmem((2 * rank, chunk), BF16),
            vmem(query_up_factor.shape, BF16),
            vmem(value_up_factor.shape, BF16),
            vmem((1, HD), F32),
            vmem((peers, HD), F32),
            vmem((1, HD), jnp.int32),
            pltpu.SMEM((1, HD), jnp.int32),
            vmem((ranks, steps * slots, 2 * rank), BF16),
            vmem((steps * slots, 2 * rank), BF16),
            vmem((peers, HD), F32),
            vmem((peers * ROWS, ROWS * slots), BF16),
            vmem((ROWS * slots, peers * ROWS), BF16),
            vmem((peers, ROWS, HD), BF16),
            vmem((peers, ROWS, HD), BF16),
            vmem((peers, ROWS, HD), BF16),
            vmem((peers, ROWS, HD), BF16),
            vmem((ROWS * slots, HD), F32),
            vmem((slots, HD), F32),
            vmem((slots, HD), F32),
            vmem((peers, HD), F32),
            vmem((peers * ROWS, HD), BF16),
            dma((13,)),
            dma,
            dma((3,)),
            dma((1,)),
            dma((2, 8)),
            dma((4,)),
            dma((4,)),
            pltpu.SemaphoreType.REGULAR,
            pltpu.SemaphoreType.REGULAR,
        ],
        compiler_params=pltpu.CompilerParams(
            collective_id=0, has_side_effects=True, vmem_limit_bytes=64 * 1024 * 1024
        ),
    )(
        x_rows,
        query_base_rows,
        k_base,
        value_base_rows,
        k_pool,
        v_pool,
        block_dest,
        block_slot,
        block_fill,
        a_query,
        query_up_factor,
        a_value,
        value_up_factor,
    )


def solution(mesh):
    return jax.shard_map(
        on_device,
        mesh=mesh,
        in_specs=(
            P(None, "roll", None),
            P(None, "roll", "learn"),
            P(None, "roll", "learn"),
            P(None, "roll", "learn"),
            P("roll", None, "learn"),
            P("roll", None, "learn"),
            P("roll", None),
            P("roll"),
            P("roll"),
            P("learn", None),
            P(None, "learn"),
            P("learn", None),
            P(None, "learn"),
        ),
        out_specs=P(None, "roll", "learn"),
        check_vma=False,
    )
```

```python
import functools
import math

import jax
import jax.numpy as jnp
from jax import lax
from jax.experimental import pallas as pl
from jax.experimental.pallas import tpu as pltpu
from jax.sharding import PartitionSpec as P

MESH = pl.DeviceIdType.MESH
F32 = jnp.float32
BF16 = jnp.bfloat16
HD = 128
ROWS = 16
adapter_scale = 0.5
masked_score = -1e30
no_slot = -1000.0


def iota(shape, dim):
    return lax.broadcasted_iota(jnp.int32, shape, dim)


def in_spare_row(column, tiles):
    n = column.shape[0]
    row, lane = lax.rem(iota((n, HD), 0), ROWS), iota((n, HD), 1)
    high = column.astype(BF16).astype(F32)
    middle = (column - high).astype(BF16).astype(F32)
    low = column - high - middle
    spread = jnp.where(lane == row, high, 0.0)
    spread = jnp.where(lane == row + ROWS, middle, spread)
    spread = jnp.where(lane == row + 2 * ROWS, low, spread)
    line = jnp.sum(spread.reshape(n // ROWS, ROWS, HD), axis=1, keepdims=True)
    tiles = tiles.reshape(n // ROWS, ROWS, HD)
    return jnp.where(iota(tiles.shape, 1) == ROWS - 1, line, tiles)


def kernel(
    peers,
    ranks,
    dims,
    x_hbm,
    qb_hbm,
    kb_hbm,
    vb_hbm,
    kp_hbm,
    vp_hbm,
    dest_hbm,
    slot_hbm,
    fill_hbm,
    aq_hbm,
    qu_hbm,
    av_hbm,
    vu_hbm,
    out_ref,
    x,
    dest,
    slot,
    fill,
    qb,
    kb,
    vb,
    kp,
    vp,
    a_both,
    qu,
    vu,
    tag_send,
    tag_recv,
    lane_vec,
    lane_blk,
    low_recv,
    low_total,
    tagc,
    sel,
    sel_t,
    q_send,
    q_recv,
    p_send,
    p_recv,
    new_mixed,
    top_s,
    den_s,
    wide,
    weighted,
    local_sem,
    blk_sem,
    send_sem,
    recv_sem,
    group_sem,
    low_send_sem,
    low_recv_sem,
    inner_in,
    roll_in,
):
    steps, slots, chunk, pool, block_len, group = dims
    rows = steps * group
    rank = aq_hbm.shape[0]
    me, ml = lax.axis_index("roll"), lax.axis_index("learn")
    others = pl.ds(0, peers - 1)

    chips = ranks // 2
    chip, core = ml // 2, lax.rem(ml, 2)
    partner = ml + 1 - 2 * core
    is_inner, is_outer = chip == 0, chip > 0
    is_outer0 = jnp.logical_and(is_outer, core == 0)
    is_outer1 = jnp.logical_and(is_outer, core == 1)
    n_inner = 2
    barrier = pltpu.get_barrier_semaphore()
    gatherer = ml - core * ((chip + chips - 1) // chips)

    start = pl.multiple_of(ml * chunk, HD)
    pairs = [
        (x_hbm.at[:, :, pl.ds(start, chunk)], x),
        (aq_hbm, a_both.at[pl.ds(0, rank)]),
        (av_hbm, a_both.at[pl.ds(rank, rank)]),
        (qb_hbm, qb),
        (qu_hbm, qu),
        (kb_hbm, kb),
        (vb_hbm, vb),
        (vu_hbm, vu),
        (kp_hbm, kp),
        (vp_hbm, vp),
        (dest_hbm, dest),
        (slot_hbm, slot),
        (fill_hbm, fill),
    ]
    loads = [pltpu.make_async_copy(a, b, local_sem.at[i]) for i, (a, b) in enumerate(pairs)]
    for load in loads[:3]:
        load.start()

    def signal(sem, roll, learn):
        pl.semaphore_signal(sem, inc=1, device_id=(roll, learn), device_id_type=MESH)

    def greet(i, carry):
        signal(barrier, lax.rem(me + i, peers), gatherer)
        return carry

    signal(barrier, me, partner)

    @pl.when(is_inner)
    def _():
        for j in range(1, chips):
            signal(barrier, me, 2 * j + 1)

    @pl.when(is_inner)
    def _():
        lax.fori_loop(1, peers, greet, 0, unroll=7)

    for load in loads[3:]:
        load.start()

    half = steps * slots // 2
    urgent = 2 * ROWS

    def packed(low):
        return jnp.concatenate([low[:half], low[half:]], axis=1)

    def unpacked(low):
        return jnp.concatenate([low[:, :rank], low[:, rank:]], axis=0).astype(BF16)

    def make_partial():
        for load in loads[:3]:
            load.wait()
        partial = lax.dot_general(
            x[...].reshape(steps * slots, chunk),
            a_both[...],
            (((1,), (1,)), ((), ())),
            preferred_element_type=F32,
        )
        both = jnp.concatenate([packed(partial[:, :rank]), packed(partial[:, rank:])], axis=0)
        low_recv[ml] = both.astype(BF16)

    def to_learn(src, dst, k, learn):
        return pltpu.make_async_remote_copy(
            src_ref=src,
            dst_ref=dst,
            send_sem=low_send_sem.at[k],
            recv_sem=low_recv_sem.at[k],
            device_id=(me, learn),
            device_id_type=MESH,
        )

    low_parts = [pl.ds(0, urgent), pl.ds(urgent, steps * slots - urgent)]

    def send_partial(k, targets):
        mine = low_recv.at[ml, low_parts[k]]
        for target in targets:
            to_learn(mine, mine, k, target).start()

    @pl.when(is_outer)
    def _():
        make_partial()

    @pl.when(is_outer1)
    def _():
        pl.semaphore_wait(barrier, n_inner + 1)
        signal(inner_in, me, partner)

    @pl.when(is_outer0)
    def _():
        pl.semaphore_wait(inner_in, 1)

    @pl.when(is_outer)
    def _():
        send_partial(0, range(n_inner))
        lax.fori_loop(1, peers, greet, 0, unroll=7)

    for load in loads[10:12]:
        load.wait()
    lane = iota((1, HD), 1)
    tag_row = jnp.full((1, HD), no_slot, F32)
    blk_row = jnp.zeros((1, HD), jnp.int32)
    for b in range(pool):
        hit = lane == dest[0, b]
        tag_row = jnp.where(hit, slot[b].astype(F32), tag_row)
        blk_row = jnp.where(hit, b, blk_row)
    tag_send[...] = tag_row
    tag_recv[pl.ds(me, 1), :] = tag_row
    lane_vec[...] = blk_row
    to_smem = pltpu.make_async_copy(lane_vec, lane_blk, blk_sem)
    to_smem.start()

    @pl.when(is_inner)
    def _():
        make_partial()
        pl.semaphore_wait(barrier, peers)

    @pl.when(is_outer0)
    def _():
        pl.semaphore_wait(barrier, 2 * peers - 1)
        signal(roll_in, me, partner)

    @pl.when(is_outer1)
    def _():
        pl.semaphore_wait(roll_in, 1)

    def to_roll(src_of, dst, k):
        def one(i, carry):
            d = lax.rem(me + i, peers)
            pltpu.make_async_remote_copy(
                src_ref=src_of(d),
                dst_ref=dst,
                send_sem=send_sem.at[k],
                recv_sem=recv_sem.at[k],
                device_id=(d, ml),
                device_id_type=MESH,
            ).start()
            return carry

        lax.fori_loop(1, peers, one, 0)

    side = 4
    plane = side * side
    my_y, my_z, my_x = me // plane, lax.rem(me // side, side), lax.rem(me, side)
    z_of = [my_z, my_z + 1 - 2 * lax.rem(my_z, 2), lax.rem(my_z + 2, side), side - 1 - my_z]

    y_at = [lax.rem(my_y + k, side) * plane for k in range(side)]
    z_at = [z * side for z in z_of]
    x_at = [lax.rem(my_x + k, side) for k in range(side)]

    def lane_at(c, i):
        over = 2 * (i // side) % side + i // (2 * side)
        return y_at[over] + z_at[c] + x_at[i % side]

    batch = 8
    groups = [(c, f) for c in range(side) for f in range(0, plane, batch)]

    def lanes_of(group):
        c, f = group
        return [lane_at(c, f + j) for j in range(batch)]

    def to_group(group, src, dst, k):
        c, f = group
        n = (c * plane + f) // batch

        for j in range(int(n == 0), batch):
            d = lane_at(c, f + j)
            pltpu.make_async_remote_copy(
                src_ref=src.at[n * batch + j],
                dst_ref=dst.at[me],
                send_sem=send_sem.at[k],
                recv_sem=group_sem.at[k - 1, n],
                device_id=(d, ml),
                device_id_type=MESH,
            ).start()

    def wait_group(group, buf, k):
        c, f = group
        n = (c * plane + f) // batch
        wait_for(buf.at[pl.ds(0, batch - int(n == 0))], group_sem.at[k - 1, n])

    to_roll(lambda d: tag_send, tag_recv.at[pl.ds(me, 1), :], 0)


    @pl.when(is_inner)
    def _():
        send_partial(0, [partner])
        send_partial(1, [partner])

    @pl.when(is_outer)
    def _():
        send_partial(1, range(n_inner))

    def wait_lanes(buf, sem):
        pltpu.make_async_copy(buf.at[others], buf.at[others], sem).wait()

    def wait_for(ref, sem):
        pltpu.make_async_copy(ref, ref, sem).wait()

    wait_lanes(tag_recv, recv_sem.at[0])
    mine = iota((peers, HD), 1) == me
    asked = jnp.sum(jnp.where(mine, tag_recv[...], 0.0), axis=1, keepdims=True)
    tagc[...] = jnp.broadcast_to(asked, (peers, HD))

    width = ROWS * slots
    sel_row = (iota((ROWS, width), 0) * slots).astype(F32)
    sel_lane = iota((ROWS, width), 1).astype(F32)

    def pick(c, i):
        row = tagc[pl.ds(lane_at(c, i), 1), :]
        want = sel_row + jnp.concatenate([row] * (width // HD), axis=1)
        hot = jnp.where(want == sel_lane, 1.0, 0.0).astype(BF16)
        sel[pl.ds((c * plane + i) * ROWS, ROWS), :] = hot

    for c in range(side):
        for i in range(plane):
            pick(c, i)

    for load in loads[3:5]:
        load.wait()

    def sum_part(k):
        at = low_parts[k]

        @pl.when(is_inner)
        def _():
            wait_for(low_recv.at[pl.ds(0, ranks - 1), at], low_recv_sem.at[k])
            summed = functools.reduce(
                jnp.add, [low_recv[j, at, :].astype(F32) for j in range(ranks)]
            )
            low_total[at, :] = summed.astype(BF16)
            total = low_total.at[at]
            for j in range(1, chips):
                to_learn(total, total, k + 2, 2 * j + core).start()

        @pl.when(is_outer)
        def _():
            wait_for(low_total.at[at], low_recv_sem.at[k + 2])

    sum_part(0)
    low_q = unpacked(low_total[:urgent, :].astype(F32)[:half])
    up = jnp.dot(low_q, qu[...], preferred_element_type=F32)
    query = qb[...].reshape(steps * slots, group * HD).astype(F32) + adapter_scale * up
    query = query.astype(BF16)
    tiles = [
        query[t * slots : (t + 1) * slots, g * HD : (g + 1) * HD]
        for t in range(steps)
        for g in range(group)
    ]
    stack = jnp.concatenate(tiles + [jnp.zeros((slots, HD), BF16)] * (ROWS - rows), axis=0)
    for c in range(side):
        mine = pl.ds(c * plane * ROWS, plane * ROWS)
        picked = jnp.dot(sel[mine, :], stack, preferred_element_type=F32).astype(BF16)
        q_send[pl.ds(c * plane, plane)] = picked.reshape(plane, ROWS, HD)
        for f in range(0, plane, batch):
            to_group((c, f), q_send, q_recv, 1)
    q_recv[me] = q_send[0]

    sum_part(1)
    sel_t[...] = sel[...].T

    for load in loads[8:10] + loads[12:]:
        load.wait()
    to_smem.wait()
    scale = 1.0 / math.sqrt(HD)
    token = iota((ROWS, block_len), 1)

    def some_lanes(group):
        lanes = lanes_of(group)
        first = group[0] * plane + group[1]
        blocks = [lane_blk[0, d] for d in lanes]
        scored = []
        for j in range(0, batch, 2):
            queries = jnp.concatenate([q_recv[d] for d in lanes[j : j + 2]], axis=0)
            keys = jnp.concatenate([kp[b] for b in blocks[j : j + 2]], axis=0)
            s = lax.dot_general(
                queries, keys, (((1,), (1,)), ((), ())), preferred_element_type=F32
            )
            for h in range(2):
                own = s[h * ROWS : (h + 1) * ROWS, h * block_len : (h + 1) * block_len]
                scored.append(jnp.where(token < fill[blocks[j + h]], own * scale, masked_score))
        s = jnp.concatenate(scored, axis=0)
        peak = jnp.max(s, axis=1, keepdims=True)
        w = jnp.exp(s - peak)
        total = jnp.sum(w, axis=1, keepdims=True)
        w16 = w.astype(BF16)
        mixed = []
        for j in range(0, batch, 2):
            values = jnp.concatenate([vp[b] for b in blocks[j : j + 2]], axis=1)
            m = jnp.dot(w16[j * ROWS : (j + 2) * ROWS], values, preferred_element_type=F32)
            mixed += [m[:ROWS, :HD], m[ROWS:, HD:]]
        mixed = jnp.concatenate(mixed, axis=0)
        tiles = in_spare_row(peak + jnp.log(total), mixed / total).astype(BF16)
        p_send[pl.ds(first, batch)] = tiles

    for lanes_group in groups:
        wait_group(lanes_group, q_recv, 1)
        some_lanes(lanes_group)
        to_group(lanes_group, p_send, p_recv, 2)
    p_recv[me] = p_send[0]

    for load in loads[5:8]:
        load.wait()
    low_v = unpacked(low_total[...].astype(F32)[half:])
    up_v = jnp.dot(low_v, vu[...], preferred_element_type=F32)
    value = vb[...].reshape(steps * slots, HD).astype(F32) + adapter_scale * up_v
    value = value.astype(BF16).astype(F32)
    values = [value[t * slots : (t + 1) * slots] for t in range(steps)]
    keys = [kb[t].astype(F32) for t in range(steps)]
    lane_s = iota((slots, HD), 1)
    scores = [jnp.full((slots, HD), masked_score, F32) for _ in range(steps)]
    for r in range(rows):
        q_r = tiles[r].astype(F32)
        for u in range(r // group + 1):
            s = jnp.sum(q_r * keys[u], axis=1, keepdims=True) * scale
            scores[u] = jnp.where(lane_s == r, s, scores[u])
    new_peak = functools.reduce(jnp.maximum, scores)
    new_w = [
        jnp.where(lane_s >= u * group, jnp.exp(scores[u] - new_peak), 0.0) for u in range(steps)
    ]
    new_total = functools.reduce(jnp.add, new_w)
    rounded = [w.astype(BF16).astype(F32) for w in new_w]
    for r in range(rows):
        acc = jnp.zeros((slots, HD), F32)
        for u in range(r // group + 1):
            acc = acc + rounded[u][:, r : r + 1] * values[u]
        new_mixed[pl.ds(r * slots, slots), :] = acc

    def spare_row(c, i):
        d = lane_at(c, i)
        wide[pl.ds(d, 1), :] = p_recv[d].astype(F32)[ROWS - 1 :]

    for c, f in groups:
        wait_group((c, f), p_recv, 2)
        for i in range(f, f + batch):
            spare_row(c, i)
    tags = tagc[...]
    line = wide[...]
    middle, low = pltpu.roll(line, HD - ROWS, 1), pltpu.roll(line, HD - 2 * ROWS, 1)
    lse = jnp.where(tags >= 0.0, line + middle + low, masked_score)
    for s in range(slots):
        mine_s = jnp.where(tags == float(s), lse, masked_score)
        top_s[pl.ds(s, 1), :] = jnp.max(mine_s, axis=0, keepdims=True)
    top = jnp.maximum(top_s[...], new_peak)
    top_s[...] = top
    lane_top = jnp.zeros((peers, HD), F32)
    for s in range(slots):
        lane_top = jnp.where(tags == float(s), top_s[pl.ds(s, 1), :], lane_top)
    weight = jnp.exp(lse - lane_top)
    for s in range(slots):
        mine_s = jnp.where(tags == float(s), weight, 0.0)
        den_s[pl.ds(s, 1), :] = jnp.sum(mine_s, axis=0, keepdims=True)
    new_weight = jnp.exp(new_peak - top)
    inverse = 1.0 / (den_s[...] + new_total * new_weight)
    wide[...] = weight
    on_row = iota((ROWS, HD), 0) == iota((ROWS, HD), 1)

    def weigh(c, i):
        d = lane_at(c, i)
        row = jnp.where(on_row, wide[pl.ds(d, 1), :], 0.0)
        column = jnp.sum(row, axis=1, keepdims=True)
        at = pl.ds((c * plane + i) * ROWS, ROWS)
        weighted[at, :] = (p_recv[d].astype(F32) * column).astype(BF16)

    for c in range(side):
        for i in range(plane):
            weigh(c, i)
    mixed = jnp.dot(sel_t[...], weighted[...], preferred_element_type=F32)
    for r in range(rows):
        t, g = r // group, r % group
        at = slice(r * slots, (r + 1) * slots)
        res = mixed[at] + new_weight[:, r : r + 1] * new_mixed[at, :]
        res = res * inverse[:, r : r + 1]
        out_ref[t, :, g * HD : (g + 1) * HD] = res.astype(BF16)

    @pl.when(is_inner)
    def _():
        for k in range(2):
            wait_for(low_recv.at[0, low_parts[k]], low_send_sem.at[k])
            wait_for(low_recv.at[pl.ds(0, chips - 1), low_parts[k]], low_send_sem.at[k + 2])

    @pl.when(is_outer)
    def _():
        for k in range(2):
            wait_for(low_recv.at[pl.ds(0, n_inner), low_parts[k]], low_send_sem.at[k])

    wait_lanes(tag_recv, send_sem.at[0])
    wait_lanes(q_recv, send_sem.at[1])
    wait_lanes(p_recv, send_sem.at[2])


def on_device(
    x_rows,
    query_base_rows,
    k_base,
    value_base_rows,
    k_pool,
    v_pool,
    block_dest,
    block_slot,
    block_fill,
    a_query,
    query_up_factor,
    a_value,
    value_up_factor,
):
    peers, ranks = lax.axis_size("roll"), lax.axis_size("learn")
    steps, slots, width = x_rows.shape
    pool, block_len, _ = k_pool.shape
    rank = a_query.shape[1]
    a_query, a_value, block_dest = a_query.T, a_value.T, block_dest.T
    group = query_base_rows.shape[2] // HD
    chunk = width // ranks
    dims = (steps, slots, chunk, pool, block_len, group)
    hbm = pl.BlockSpec(memory_space=pltpu.HBM)
    vmem = pltpu.VMEM
    dma = pltpu.SemaphoreType.DMA
    return pl.pallas_call(
        functools.partial(kernel, peers, ranks, dims),
        out_shape=jax.ShapeDtypeStruct(query_base_rows.shape, BF16),
        in_specs=[hbm] * 13,
        out_specs=pl.BlockSpec(memory_space=pltpu.VMEM),
        scratch_shapes=[
            vmem((steps, slots, chunk), BF16),
            pltpu.SMEM(block_dest.shape, jnp.int32),
            pltpu.SMEM(block_slot.shape, jnp.int32),
            pltpu.SMEM(block_fill.shape, jnp.int32),
            vmem(query_base_rows.shape, BF16),
            vmem(k_base.shape, BF16),
            vmem(value_base_rows.shape, BF16),
            vmem(k_pool.shape, BF16),
            vmem(v_pool.shape, BF16),
            vmem((2 * rank, chunk), BF16),
            vmem(query_up_factor.shape, BF16),
            vmem(value_up_factor.shape, BF16),
            vmem((1, HD), F32),
            vmem((peers, HD), F32),
            vmem((1, HD), jnp.int32),
            pltpu.SMEM((1, HD), jnp.int32),
            vmem((ranks, steps * slots, 2 * rank), BF16),
            vmem((steps * slots, 2 * rank), BF16),
            vmem((peers, HD), F32),
            vmem((peers * ROWS, ROWS * slots), BF16),
            vmem((ROWS * slots, peers * ROWS), BF16),
            vmem((peers, ROWS, HD), BF16),
            vmem((peers, ROWS, HD), BF16),
            vmem((peers, ROWS, HD), BF16),
            vmem((peers, ROWS, HD), BF16),
            vmem((ROWS * slots, HD), F32),
            vmem((slots, HD), F32),
            vmem((slots, HD), F32),
            vmem((peers, HD), F32),
            vmem((peers * ROWS, HD), BF16),
            dma((13,)),
            dma,
            dma((3,)),
            dma((1,)),
            dma((2, 8)),
            dma((4,)),
            dma((4,)),
            pltpu.SemaphoreType.REGULAR,
            pltpu.SemaphoreType.REGULAR,
        ],
        compiler_params=pltpu.CompilerParams(
            collective_id=0, has_side_effects=True, vmem_limit_bytes=64 * 1024 * 1024
        ),
    )(
        x_rows,
        query_base_rows,
        k_base,
        value_base_rows,
        k_pool,
        v_pool,
        block_dest,
        block_slot,
        block_fill,
        a_query,
        query_up_factor,
        a_value,
        value_up_factor,
    )


def solution(mesh):
    return jax.shard_map(
        on_device,
        mesh=mesh,
        in_specs=(
            P(None, "roll", None),
            P(None, "roll", "learn"),
            P(None, "roll", "learn"),
            P(None, "roll", "learn"),
            P("roll", None, "learn"),
            P("roll", None, "learn"),
            P("roll", None),
            P("roll"),
            P("roll"),
            P("learn", None),
            P(None, "learn"),
            P("learn", None),
            P(None, "learn"),
        ),
        out_specs=P(None, "roll", "learn"),
        check_vma=False,
    )
```

```python
import functools
import math

import jax
import jax.numpy as jnp
from jax import lax
from jax.experimental import pallas as pl
from jax.experimental.pallas import tpu as pltpu
from jax.sharding import PartitionSpec as P

MESH = pl.DeviceIdType.MESH
F32 = jnp.float32
BF16 = jnp.bfloat16
HD = 128
ROWS = 16
adapter_scale = 0.5
masked_score = -1e30
no_slot = -1000.0


def iota(shape, dim):
    return lax.broadcasted_iota(jnp.int32, shape, dim)


def in_spare_row(column, tiles):
    n = column.shape[0]
    row, lane = lax.rem(iota((n, HD), 0), ROWS), iota((n, HD), 1)
    high = column.astype(BF16).astype(F32)
    middle = (column - high).astype(BF16).astype(F32)
    low = column - high - middle
    spread = jnp.where(lane == row, high, 0.0)
    spread = jnp.where(lane == row + ROWS, middle, spread)
    spread = jnp.where(lane == row + 2 * ROWS, low, spread)
    line = jnp.sum(spread.reshape(n // ROWS, ROWS, HD), axis=1, keepdims=True)
    tiles = tiles.reshape(n // ROWS, ROWS, HD)
    return jnp.where(iota(tiles.shape, 1) == ROWS - 1, line, tiles)


def kernel(
    peers,
    ranks,
    dims,
    x_hbm,
    qb_hbm,
    kb_hbm,
    vb_hbm,
    kp_hbm,
    vp_hbm,
    dest_hbm,
    slot_hbm,
    fill_hbm,
    aq_hbm,
    qu_hbm,
    av_hbm,
    vu_hbm,
    out_ref,
    x,
    dest,
    slot,
    fill,
    qb,
    kb,
    vb,
    kp,
    vp,
    a_both,
    qu,
    vu,
    tag_send,
    tag_recv,
    lane_vec,
    lane_blk,
    low_recv,
    low_total,
    tagc,
    sel,
    sel_t,
    q_send,
    q_recv,
    p_send,
    p_recv,
    new_mixed,
    top_s,
    den_s,
    wide,
    weighted,
    local_sem,
    blk_sem,
    send_sem,
    recv_sem,
    group_sem,
    low_send_sem,
    low_recv_sem,
    inner_in,
    roll_in,
):
    steps, slots, chunk, pool, block_len, group = dims
    rows = steps * group
    rank = aq_hbm.shape[0]
    me, ml = lax.axis_index("roll"), lax.axis_index("learn")
    others = pl.ds(0, peers - 1)

    chips = ranks // 2
    chip, core = ml // 2, lax.rem(ml, 2)
    partner = ml + 1 - 2 * core
    is_inner, is_outer = chip == 0, chip > 0
    is_outer0 = jnp.logical_and(is_outer, core == 0)
    is_outer1 = jnp.logical_and(is_outer, core == 1)
    n_inner = 2
    barrier = pltpu.get_barrier_semaphore()
    gatherer = ml - core * ((chip + chips - 1) // chips)

    start = pl.multiple_of(ml * chunk, HD)
    pairs = [
        (x_hbm.at[:, :, pl.ds(start, chunk)], x),
        (aq_hbm, a_both.at[pl.ds(0, rank)]),
        (av_hbm, a_both.at[pl.ds(rank, rank)]),
        (qb_hbm, qb),
        (qu_hbm, qu),
        (kb_hbm, kb),
        (vb_hbm, vb),
        (vu_hbm, vu),
        (kp_hbm, kp),
        (vp_hbm, vp),
        (dest_hbm, dest),
        (slot_hbm, slot),
        (fill_hbm, fill),
    ]
    loads = [pltpu.make_async_copy(a, b, local_sem.at[i]) for i, (a, b) in enumerate(pairs)]
    for load in loads[:3]:
        load.start()

    def signal(sem, roll, learn):
        pl.semaphore_signal(sem, inc=1, device_id=(roll, learn), device_id_type=MESH)

    def greet(i, carry):
        signal(barrier, lax.rem(me + i, peers), gatherer)
        return carry

    signal(barrier, me, partner)

    @pl.when(is_inner)
    def _():
        for j in range(1, chips):
            signal(barrier, me, 2 * j + 1)

    @pl.when(is_inner)
    def _():
        lax.fori_loop(1, peers, greet, 0, unroll=7)

    for load in loads[3:]:
        load.start()

    half = steps * slots // 2
    urgent = 2 * ROWS

    def packed(low):
        return jnp.concatenate([low[:half], low[half:]], axis=1)

    def unpacked(low):
        return jnp.concatenate([low[:, :rank], low[:, rank:]], axis=0).astype(BF16)

    def make_partial():
        for load in loads[:3]:
            load.wait()
        partial = lax.dot_general(
            x[...].reshape(steps * slots, chunk),
            a_both[...],
            (((1,), (1,)), ((), ())),
            preferred_element_type=F32,
        )
        both = jnp.concatenate([packed(partial[:, :rank]), packed(partial[:, rank:])], axis=0)
        low_recv[ml] = both.astype(BF16)

    def to_learn(src, dst, k, learn):
        return pltpu.make_async_remote_copy(
            src_ref=src,
            dst_ref=dst,
            send_sem=low_send_sem.at[k],
            recv_sem=low_recv_sem.at[k],
            device_id=(me, learn),
            device_id_type=MESH,
        )

    low_parts = [pl.ds(0, urgent), pl.ds(urgent, steps * slots - urgent)]

    def send_partial(k, targets):
        mine = low_recv.at[ml, low_parts[k]]
        for target in targets:
            to_learn(mine, mine, k, target).start()

    @pl.when(is_outer)
    def _():
        make_partial()

    @pl.when(is_outer1)
    def _():
        pl.semaphore_wait(barrier, n_inner + 1)
        signal(inner_in, me, partner)

    @pl.when(is_outer0)
    def _():
        pl.semaphore_wait(inner_in, 1)

    @pl.when(is_outer)
    def _():
        send_partial(0, range(n_inner))
        lax.fori_loop(1, peers, greet, 0, unroll=7)

    for load in loads[10:12]:
        load.wait()
    lane = iota((1, HD), 1)
    tag_row = jnp.full((1, HD), no_slot, F32)
    blk_row = jnp.zeros((1, HD), jnp.int32)
    for b in range(pool):
        hit = lane == dest[0, b]
        tag_row = jnp.where(hit, slot[b].astype(F32), tag_row)
        blk_row = jnp.where(hit, b, blk_row)
    tag_send[...] = tag_row
    tag_recv[pl.ds(me, 1), :] = tag_row
    lane_vec[...] = blk_row
    to_smem = pltpu.make_async_copy(lane_vec, lane_blk, blk_sem)
    to_smem.start()

    @pl.when(is_inner)
    def _():
        make_partial()
        pl.semaphore_wait(barrier, peers)

    @pl.when(is_outer0)
    def _():
        pl.semaphore_wait(barrier, 2 * peers - 1)
        signal(roll_in, me, partner)

    @pl.when(is_outer1)
    def _():
        pl.semaphore_wait(roll_in, 1)

    def to_roll(src_of, dst, k):
        def one(i, carry):
            d = lax.rem(me + i, peers)
            pltpu.make_async_remote_copy(
                src_ref=src_of(d),
                dst_ref=dst,
                send_sem=send_sem.at[k],
                recv_sem=recv_sem.at[k],
                device_id=(d, ml),
                device_id_type=MESH,
            ).start()
            return carry

        lax.fori_loop(1, peers, one, 0)

    side = 4
    plane = side * side
    my_y, my_z, my_x = me // plane, lax.rem(me // side, side), lax.rem(me, side)
    z_of = [my_z, my_z + 1 - 2 * lax.rem(my_z, 2), lax.rem(my_z + 2, side), side - 1 - my_z]

    y_at = [lax.rem(my_y + k, side) * plane for k in range(side)]
    z_at = [z * side for z in z_of]
    x_at = [lax.rem(my_x + k, side) for k in range(side)]

    def lane_at(c, i):
        over = 2 * (i // side) % side + i // (2 * side)
        return y_at[over] + z_at[c] + x_at[i % side]

    batch = 8
    groups = [(c, f) for c in range(side) for f in range(0, plane, batch)]

    def lanes_of(group):
        c, f = group
        return [lane_at(c, f + j) for j in range(batch)]

    def to_group(group, src, dst, k):
        c, f = group
        n = (c * plane + f) // batch

        for j in range(int(n == 0), batch):
            d = lane_at(c, f + j)
            pltpu.make_async_remote_copy(
                src_ref=src.at[n * batch + j],
                dst_ref=dst.at[me],
                send_sem=send_sem.at[k],
                recv_sem=group_sem.at[k - 1, n],
                device_id=(d, ml),
                device_id_type=MESH,
            ).start()

    def wait_group(group, buf, k):
        c, f = group
        n = (c * plane + f) // batch
        wait_for(buf.at[pl.ds(0, batch - int(n == 0))], group_sem.at[k - 1, n])

    to_roll(lambda d: tag_send, tag_recv.at[pl.ds(me, 1), :], 0)


    @pl.when(is_inner)
    def _():
        send_partial(0, [partner])
        send_partial(1, [partner])

    @pl.when(is_outer)
    def _():
        send_partial(1, range(n_inner))

    def wait_lanes(buf, sem):
        pltpu.make_async_copy(buf.at[others], buf.at[others], sem).wait()

    def wait_for(ref, sem):
        pltpu.make_async_copy(ref, ref, sem).wait()

    wait_lanes(tag_recv, recv_sem.at[0])
    mine = iota((peers, HD), 1) == me
    asked = jnp.sum(jnp.where(mine, tag_recv[...], 0.0), axis=1, keepdims=True)
    tagc[...] = jnp.broadcast_to(asked, (peers, HD))

    width = ROWS * slots
    sel_row = (iota((ROWS, width), 0) * slots).astype(F32)
    sel_lane = iota((ROWS, width), 1).astype(F32)

    def pick(c, i):
        row = tagc[pl.ds(lane_at(c, i), 1), :]
        want = sel_row + jnp.concatenate([row] * (width // HD), axis=1)
        hot = jnp.where(want == sel_lane, 1.0, 0.0).astype(BF16)
        sel[pl.ds((c * plane + i) * ROWS, ROWS), :] = hot

    for c in range(side):
        for i in range(plane):
            pick(c, i)

    for load in loads[3:5]:
        load.wait()

    def sum_part(k):
        at = low_parts[k]

        @pl.when(is_inner)
        def _():
            wait_for(low_recv.at[pl.ds(0, ranks - 1), at], low_recv_sem.at[k])
            summed = functools.reduce(
                jnp.add, [low_recv[j, at, :].astype(F32) for j in range(ranks)]
            )
            low_total[at, :] = summed.astype(BF16)
            total = low_total.at[at]
            for j in range(1, chips):
                to_learn(total, total, k + 2, 2 * j + core).start()

        @pl.when(is_outer)
        def _():
            wait_for(low_total.at[at], low_recv_sem.at[k + 2])

    sum_part(0)
    low_q = unpacked(low_total[:urgent, :].astype(F32)[:half])
    up = jnp.dot(low_q, qu[...], preferred_element_type=F32)
    query = qb[...].reshape(steps * slots, group * HD).astype(F32) + adapter_scale * up
    query = query.astype(BF16)
    tiles = [
        query[t * slots : (t + 1) * slots, g * HD : (g + 1) * HD]
        for t in range(steps)
        for g in range(group)
    ]
    stack = jnp.concatenate(tiles + [jnp.zeros((slots, HD), BF16)] * (ROWS - rows), axis=0)
    for c in range(side):
        mine = pl.ds(c * plane * ROWS, plane * ROWS)
        picked = jnp.dot(sel[mine, :], stack, preferred_element_type=F32).astype(BF16)
        q_send[pl.ds(c * plane, plane)] = picked.reshape(plane, ROWS, HD)
        for f in range(0, plane, batch):
            to_group((c, f), q_send, q_recv, 1)
    q_recv[me] = q_send[0]

    sum_part(1)
    sel_t[...] = sel[...].T

    for load in loads[8:10] + loads[12:]:
        load.wait()
    to_smem.wait()
    scale = 1.0 / math.sqrt(HD)
    token = iota((ROWS, block_len), 1)

    def some_lanes(group):
        lanes = lanes_of(group)
        first = group[0] * plane + group[1]
        blocks = [lane_blk[0, d] for d in lanes]
        scored = []
        for j in range(0, batch, 2):
            queries = jnp.concatenate([q_recv[d] for d in lanes[j : j + 2]], axis=0)
            keys = jnp.concatenate([kp[b] for b in blocks[j : j + 2]], axis=0)
            s = lax.dot_general(
                queries, keys, (((1,), (1,)), ((), ())), preferred_element_type=F32
            )
            for h in range(2):
                own = s[h * ROWS : (h + 1) * ROWS, h * block_len : (h + 1) * block_len]
                scored.append(jnp.where(token < fill[blocks[j + h]], own * scale, masked_score))
        s = jnp.concatenate(scored, axis=0)
        peak = jnp.max(s, axis=1, keepdims=True)
        w = jnp.exp(s - peak)
        total = jnp.sum(w, axis=1, keepdims=True)
        w16 = w.astype(BF16)
        mixed = []
        for j in range(0, batch, 2):
            values = jnp.concatenate([vp[b] for b in blocks[j : j + 2]], axis=1)
            m = jnp.dot(w16[j * ROWS : (j + 2) * ROWS], values, preferred_element_type=F32)
            mixed += [m[:ROWS, :HD], m[ROWS:, HD:]]
        mixed = jnp.concatenate(mixed, axis=0)
        tiles = in_spare_row(peak + jnp.log(total), mixed / total).astype(BF16)
        p_send[pl.ds(first, batch)] = tiles

    for lanes_group in groups:
        wait_group(lanes_group, q_recv, 1)
        some_lanes(lanes_group)
        to_group(lanes_group, p_send, p_recv, 2)
    p_recv[me] = p_send[0]

    for load in loads[5:8]:
        load.wait()
    low_v = unpacked(low_total[...].astype(F32)[half:])
    up_v = jnp.dot(low_v, vu[...], preferred_element_type=F32)
    value = vb[...].reshape(steps * slots, HD).astype(F32) + adapter_scale * up_v
    value = value.astype(BF16).astype(F32)
    values = [value[t * slots : (t + 1) * slots] for t in range(steps)]
    keys = [kb[t].astype(F32) for t in range(steps)]
    lane_s = iota((slots, HD), 1)
    scores = [jnp.full((slots, HD), masked_score, F32) for _ in range(steps)]
    for r in range(rows):
        q_r = tiles[r].astype(F32)
        for u in range(r // group + 1):
            s = jnp.sum(q_r * keys[u], axis=1, keepdims=True) * scale
            scores[u] = jnp.where(lane_s == r, s, scores[u])
    new_peak = functools.reduce(jnp.maximum, scores)
    new_w = [
        jnp.where(lane_s >= u * group, jnp.exp(scores[u] - new_peak), 0.0) for u in range(steps)
    ]
    new_total = functools.reduce(jnp.add, new_w)
    rounded = [w.astype(BF16).astype(F32) for w in new_w]
    for r in range(rows):
        acc = jnp.zeros((slots, HD), F32)
        for u in range(r // group + 1):
            acc = acc + rounded[u][:, r : r + 1] * values[u]
        new_mixed[pl.ds(r * slots, slots), :] = acc

    def spare_row(c, i):
        d = lane_at(c, i)
        wide[pl.ds(d, 1), :] = p_recv[d].astype(F32)[ROWS - 1 :]

    for c, f in groups:
        wait_group((c, f), p_recv, 2)
        for i in range(f, f + batch):
            spare_row(c, i)
    tags = tagc[...]
    line = wide[...]
    middle, low = pltpu.roll(line, HD - ROWS, 1), pltpu.roll(line, HD - 2 * ROWS, 1)
    lse = jnp.where(tags >= 0.0, line + middle + low, masked_score)
    for s in range(slots):
        mine_s = jnp.where(tags == float(s), lse, masked_score)
        top_s[pl.ds(s, 1), :] = jnp.max(mine_s, axis=0, keepdims=True)
    top = jnp.maximum(top_s[...], new_peak)
    top_s[...] = top
    lane_top = jnp.zeros((peers, HD), F32)
    for s in range(slots):
        lane_top = jnp.where(tags == float(s), top_s[pl.ds(s, 1), :], lane_top)
    weight = jnp.exp(lse - lane_top)
    for s in range(slots):
        mine_s = jnp.where(tags == float(s), weight, 0.0)
        den_s[pl.ds(s, 1), :] = jnp.sum(mine_s, axis=0, keepdims=True)
    new_weight = jnp.exp(new_peak - top)
    inverse = 1.0 / (den_s[...] + new_total * new_weight)
    wide[...] = weight
    on_row = iota((ROWS, HD), 0) == iota((ROWS, HD), 1)

    def weigh(c, i):
        d = lane_at(c, i)
        row = jnp.where(on_row, wide[pl.ds(d, 1), :], 0.0)
        column = jnp.sum(row, axis=1, keepdims=True)
        at = pl.ds((c * plane + i) * ROWS, ROWS)
        weighted[at, :] = (p_recv[d].astype(F32) * column).astype(BF16)

    for c in range(side):
        for i in range(plane):
            weigh(c, i)
    mixed = jnp.dot(sel_t[...], weighted[...], preferred_element_type=F32)
    for r in range(rows):
        t, g = r // group, r % group
        at = slice(r * slots, (r + 1) * slots)
        res = mixed[at] + new_weight[:, r : r + 1] * new_mixed[at, :]
        res = res * inverse[:, r : r + 1]
        out_ref[t, :, g * HD : (g + 1) * HD] = res.astype(BF16)

    @pl.when(is_inner)
    def _():
        for k in range(2):
            wait_for(low_recv.at[0, low_parts[k]], low_send_sem.at[k])
            wait_for(low_recv.at[pl.ds(0, chips - 1), low_parts[k]], low_send_sem.at[k + 2])

    @pl.when(is_outer)
    def _():
        for k in range(2):
            wait_for(low_recv.at[pl.ds(0, n_inner), low_parts[k]], low_send_sem.at[k])

    wait_lanes(tag_recv, send_sem.at[0])
    wait_lanes(q_recv, send_sem.at[1])
    wait_lanes(p_recv, send_sem.at[2])


def on_device(
    x_rows,
    query_base_rows,
    k_base,
    value_base_rows,
    k_pool,
    v_pool,
    block_dest,
    block_slot,
    block_fill,
    a_query,
    query_up_factor,
    a_value,
    value_up_factor,
):
    peers, ranks = lax.axis_size("roll"), lax.axis_size("learn")
    steps, slots, width = x_rows.shape
    pool, block_len, _ = k_pool.shape
    rank = a_query.shape[1]
    a_query, a_value, block_dest = a_query.T, a_value.T, block_dest.T
    group = query_base_rows.shape[2] // HD
    chunk = width // ranks
    dims = (steps, slots, chunk, pool, block_len, group)
    hbm = pl.BlockSpec(memory_space=pltpu.HBM)
    vmem = pltpu.VMEM
    dma = pltpu.SemaphoreType.DMA
    arrays = (
        x_rows,
        query_base_rows,
        k_base,
        value_base_rows,
        k_pool,
        v_pool,
        block_dest,
        block_slot,
        block_fill,
        a_query,
        query_up_factor,
        a_value,
        value_up_factor,
    )
    return pl.pallas_call(
        functools.partial(kernel, peers, ranks, dims),
        out_shape=pltpu.VMEM(query_base_rows.shape, BF16),
        in_specs=[hbm] * 13,
        out_specs=pl.BlockSpec(memory_space=pltpu.VMEM),
        scratch_shapes=[
            vmem((steps, slots, chunk), BF16),
            pltpu.SMEM(block_dest.shape, jnp.int32),
            pltpu.SMEM(block_slot.shape, jnp.int32),
            pltpu.SMEM(block_fill.shape, jnp.int32),
            vmem(query_base_rows.shape, BF16),
            vmem(k_base.shape, BF16),
            vmem(value_base_rows.shape, BF16),
            vmem(k_pool.shape, BF16),
            vmem(v_pool.shape, BF16),
            vmem((2 * rank, chunk), BF16),
            vmem(query_up_factor.shape, BF16),
            vmem(value_up_factor.shape, BF16),
            vmem((1, HD), F32),
            vmem((peers, HD), F32),
            vmem((1, HD), jnp.int32),
            pltpu.SMEM((1, HD), jnp.int32),
            vmem((ranks, steps * slots, 2 * rank), BF16),
            vmem((steps * slots, 2 * rank), BF16),
            vmem((peers, HD), F32),
            vmem((peers * ROWS, ROWS * slots), BF16),
            vmem((ROWS * slots, peers * ROWS), BF16),
            vmem((peers, ROWS, HD), BF16),
            vmem((peers, ROWS, HD), BF16),
            vmem((peers, ROWS, HD), BF16),
            vmem((peers, ROWS, HD), BF16),
            vmem((ROWS * slots, HD), F32),
            vmem((slots, HD), F32),
            vmem((slots, HD), F32),
            vmem((peers, HD), F32),
            vmem((peers * ROWS, HD), BF16),
            dma((13,)),
            dma,
            dma((3,)),
            dma((1,)),
            dma((2, 8)),
            dma((4,)),
            dma((4,)),
            pltpu.SemaphoreType.REGULAR,
            pltpu.SemaphoreType.REGULAR,
        ],
        compiler_params=pltpu.CompilerParams(
            collective_id=0, has_side_effects=True, vmem_limit_bytes=48 * 1024 * 1024
        ),
    )(*[pltpu.with_memory_space_constraint(array, pltpu.HBM) for array in arrays])


def solution(mesh):
    return jax.shard_map(
        on_device,
        mesh=mesh,
        in_specs=(
            P(None, "roll", None),
            P(None, "roll", "learn"),
            P(None, "roll", "learn"),
            P(None, "roll", "learn"),
            P("roll", None, "learn"),
            P("roll", None, "learn"),
            P("roll", None),
            P("roll"),
            P("roll"),
            P("learn", None),
            P(None, "learn"),
            P("learn", None),
            P(None, "learn"),
        ),
        out_specs=P(None, "roll", "learn"),
        check_vma=False,
    )
```

```python
import functools
import math

import jax
import jax.numpy as jnp
from jax import lax
from jax.experimental import pallas as pl
from jax.experimental.pallas import tpu as pltpu
from jax.sharding import PartitionSpec as P

MESH = pl.DeviceIdType.MESH
F32 = jnp.float32
BF16 = jnp.bfloat16
HD = 128
ROWS = 16
adapter_scale = 0.5
masked_score = -1e30
no_slot = -1000.0


def iota(shape, dim):
    return lax.broadcasted_iota(jnp.int32, shape, dim)


def in_spare_row(column, tiles):
    n = column.shape[0]
    row, lane = lax.rem(iota((n, HD), 0), ROWS), iota((n, HD), 1)
    high = column.astype(BF16).astype(F32)
    middle = (column - high).astype(BF16).astype(F32)
    low = column - high - middle
    spread = jnp.where(lane == row, high, 0.0)
    spread = jnp.where(lane == row + ROWS, middle, spread)
    spread = jnp.where(lane == row + 2 * ROWS, low, spread)
    line = jnp.sum(spread.reshape(n // ROWS, ROWS, HD), axis=1, keepdims=True)
    tiles = tiles.reshape(n // ROWS, ROWS, HD)
    return jnp.where(iota(tiles.shape, 1) == ROWS - 1, line, tiles)


def kernel(
    peers,
    ranks,
    dims,
    x_hbm,
    qb_hbm,
    kb_hbm,
    vb_hbm,
    kp_hbm,
    vp_hbm,
    dest_hbm,
    slot_hbm,
    fill_hbm,
    aq_hbm,
    qu_hbm,
    av_hbm,
    vu_hbm,
    out_ref,
    x,
    dest,
    slot,
    fill,
    qb,
    kb,
    vb,
    kp,
    vp,
    a_both,
    qu,
    vu,
    tag_send,
    tag_recv,
    lane_vec,
    lane_blk,
    low_recv,
    low_total,
    tagc,
    sel,
    sel_t,
    q_send,
    q_recv,
    p_send,
    p_recv,
    new_mixed,
    top_s,
    den_s,
    wide,
    weighted,
    local_sem,
    blk_sem,
    send_sem,
    recv_sem,
    group_sem,
    low_send_sem,
    low_recv_sem,
    inner_in,
    roll_in,
):
    steps, slots, chunk, pool, block_len, group = dims
    rows = steps * group
    rank = aq_hbm.shape[0]
    me, ml = lax.axis_index("roll"), lax.axis_index("learn")
    others = pl.ds(0, peers - 1)

    chips = ranks // 2
    chip, core = ml // 2, lax.rem(ml, 2)
    partner = ml + 1 - 2 * core
    is_inner, is_outer = chip == 0, chip > 0
    is_outer0 = jnp.logical_and(is_outer, core == 0)
    is_outer1 = jnp.logical_and(is_outer, core == 1)
    n_inner = 2
    barrier = pltpu.get_barrier_semaphore()
    gatherer = ml - core * ((chip + chips - 1) // chips)

    start = pl.multiple_of(ml * chunk, HD)
    pairs = [
        (x_hbm.at[:, :, pl.ds(start, chunk)], x),
        (aq_hbm, a_both.at[pl.ds(0, rank)]),
        (av_hbm, a_both.at[pl.ds(rank, rank)]),
        (qb_hbm, qb),
        (qu_hbm, qu),
        (kb_hbm, kb),
        (vb_hbm, vb),
        (vu_hbm, vu),
        (kp_hbm, kp),
        (vp_hbm, vp),
        (dest_hbm, dest),
        (slot_hbm, slot),
        (fill_hbm, fill),
    ]
    loads = [pltpu.make_async_copy(a, b, local_sem.at[i]) for i, (a, b) in enumerate(pairs)]
    for load in loads[:3]:
        load.start()

    def signal(sem, roll, learn):
        pl.semaphore_signal(sem, inc=1, device_id=(roll, learn), device_id_type=MESH)

    def greet(i, carry):
        signal(barrier, lax.rem(me + i, peers), gatherer)
        return carry

    signal(barrier, me, partner)

    @pl.when(is_inner)
    def _():
        for j in range(1, chips):
            signal(barrier, me, 2 * j + 1)

    @pl.when(is_inner)
    def _():
        lax.fori_loop(1, peers, greet, 0, unroll=7)

    for load in loads[3:]:
        load.start()

    half = steps * slots // 2
    urgent = 2 * ROWS

    def packed(low):
        return jnp.concatenate([low[:half], low[half:]], axis=1)

    def unpacked(low):
        return jnp.concatenate([low[:, :rank], low[:, rank:]], axis=0).astype(BF16)

    def make_partial():
        for load in loads[:3]:
            load.wait()
        partial = lax.dot_general(
            x[...].reshape(steps * slots, chunk),
            a_both[...],
            (((1,), (1,)), ((), ())),
            preferred_element_type=F32,
        )
        both = jnp.concatenate([packed(partial[:, :rank]), packed(partial[:, rank:])], axis=0)
        low_recv[ml] = both.astype(BF16)

    def to_learn(src, dst, k, learn):
        return pltpu.make_async_remote_copy(
            src_ref=src,
            dst_ref=dst,
            send_sem=low_send_sem.at[k],
            recv_sem=low_recv_sem.at[k],
            device_id=(me, learn),
            device_id_type=MESH,
        )

    low_parts = [pl.ds(0, urgent), pl.ds(urgent, steps * slots - urgent)]

    def send_partial(k, targets):
        mine = low_recv.at[ml, low_parts[k]]
        for target in targets:
            to_learn(mine, mine, k, target).start()

    @pl.when(is_outer)
    def _():
        make_partial()

    @pl.when(is_outer1)
    def _():
        pl.semaphore_wait(barrier, n_inner + 1)
        signal(inner_in, me, partner)

    @pl.when(is_outer0)
    def _():
        pl.semaphore_wait(inner_in, 1)

    @pl.when(is_outer)
    def _():
        send_partial(0, range(n_inner))
        lax.fori_loop(1, peers, greet, 0, unroll=7)

    for load in loads[10:12]:
        load.wait()
    lane = iota((1, HD), 1)
    tag_row = jnp.full((1, HD), no_slot, F32)
    blk_row = jnp.zeros((1, HD), jnp.int32)
    for b in range(pool):
        hit = lane == dest[0, b]
        tag_row = jnp.where(hit, slot[b].astype(F32), tag_row)
        blk_row = jnp.where(hit, b, blk_row)
    tag_send[...] = tag_row
    tag_recv[pl.ds(me, 1), :] = tag_row
    lane_vec[...] = blk_row
    to_smem = pltpu.make_async_copy(lane_vec, lane_blk, blk_sem)
    to_smem.start()

    @pl.when(is_inner)
    def _():
        make_partial()
        pl.semaphore_wait(barrier, peers)

    @pl.when(is_outer0)
    def _():
        pl.semaphore_wait(barrier, 2 * peers - 1)
        signal(roll_in, me, partner)

    @pl.when(is_outer1)
    def _():
        pl.semaphore_wait(roll_in, 1)

    def to_roll(src_of, dst, k):
        def one(i, carry):
            d = lax.rem(me + i, peers)
            pltpu.make_async_remote_copy(
                src_ref=src_of(d),
                dst_ref=dst,
                send_sem=send_sem.at[k],
                recv_sem=recv_sem.at[k],
                device_id=(d, ml),
                device_id_type=MESH,
            ).start()
            return carry

        lax.fori_loop(1, peers, one, 0)

    side = 4
    plane = side * side
    my_y, my_z, my_x = me // plane, lax.rem(me // side, side), lax.rem(me, side)
    z_of = [my_z, my_z + 1 - 2 * lax.rem(my_z, 2), lax.rem(my_z + 2, side), side - 1 - my_z]

    y_at = [lax.rem(my_y + k, side) * plane for k in range(side)]
    z_at = [z * side for z in z_of]
    x_at = [lax.rem(my_x + k, side) for k in range(side)]

    def lane_at(c, i):
        over = 2 * (i // side) % side + i // (2 * side)
        return y_at[over] + z_at[c] + x_at[i % side]

    batch = 8
    groups = [(c, f) for c in range(side) for f in range(0, plane, batch)]

    def lanes_of(group):
        c, f = group
        return [lane_at(c, f + j) for j in range(batch)]

    def to_group(group, src, dst, k):
        c, f = group
        n = (c * plane + f) // batch

        for j in range(int(n == 0), batch):
            d = lane_at(c, f + j)
            pltpu.make_async_remote_copy(
                src_ref=src.at[n * batch + j],
                dst_ref=dst.at[me],
                send_sem=send_sem.at[k],
                recv_sem=group_sem.at[k - 1, n],
                device_id=(d, ml),
                device_id_type=MESH,
            ).start()

    def wait_group(group, buf, k):
        c, f = group
        n = (c * plane + f) // batch
        wait_for(buf.at[pl.ds(0, batch - int(n == 0))], group_sem.at[k - 1, n])

    to_roll(lambda d: tag_send, tag_recv.at[pl.ds(me, 1), :], 0)


    @pl.when(is_inner)
    def _():
        send_partial(0, [partner])
        send_partial(1, [partner])

    @pl.when(is_outer)
    def _():
        send_partial(1, range(n_inner))

    def wait_lanes(buf, sem):
        pltpu.make_async_copy(buf.at[others], buf.at[others], sem).wait()

    def wait_for(ref, sem):
        pltpu.make_async_copy(ref, ref, sem).wait()

    wait_lanes(tag_recv, recv_sem.at[0])
    mine = iota((peers, HD), 1) == me
    asked = jnp.sum(jnp.where(mine, tag_recv[...], 0.0), axis=1, keepdims=True)
    tagc[...] = jnp.broadcast_to(asked, (peers, HD))

    width = ROWS * slots
    sel_row = (iota((ROWS, width), 0) * slots).astype(F32)
    sel_lane = iota((ROWS, width), 1).astype(F32)

    def pick(c, i):
        row = tagc[pl.ds(lane_at(c, i), 1), :]
        want = sel_row + jnp.concatenate([row] * (width // HD), axis=1)
        hot = jnp.where(want == sel_lane, 1.0, 0.0).astype(BF16)
        sel[pl.ds((c * plane + i) * ROWS, ROWS), :] = hot

    for c in range(side):
        for i in range(plane):
            pick(c, i)

    for load in loads[3:5]:
        load.wait()

    def sum_part(k):
        at = low_parts[k]

        @pl.when(is_inner)
        def _():
            wait_for(low_recv.at[pl.ds(0, ranks - 1), at], low_recv_sem.at[k])
            summed = functools.reduce(
                jnp.add, [low_recv[j, at, :].astype(F32) for j in range(ranks)]
            )
            low_total[at, :] = summed.astype(BF16)
            total = low_total.at[at]
            for j in range(1, chips):
                to_learn(total, total, k + 2, 2 * j + core).start()

    def take_part(k):
        @pl.when(is_outer)
        def _():
            wait_for(low_total.at[low_parts[k]], low_recv_sem.at[k + 2])

    sum_part(0)
    take_part(0)
    low_q = unpacked(low_total[:urgent, :].astype(F32)[:half])
    up = jnp.dot(low_q, qu[...], preferred_element_type=F32)
    query = qb[...].reshape(steps * slots, group * HD).astype(F32) + adapter_scale * up
    query = query.astype(BF16)
    tiles = [
        query[t * slots : (t + 1) * slots, g * HD : (g + 1) * HD]
        for t in range(steps)
        for g in range(group)
    ]
    stack = jnp.concatenate(tiles + [jnp.zeros((slots, HD), BF16)] * (ROWS - rows), axis=0)
    for c in range(side):
        mine = pl.ds(c * plane * ROWS, plane * ROWS)
        picked = jnp.dot(sel[mine, :], stack, preferred_element_type=F32).astype(BF16)
        q_send[pl.ds(c * plane, plane)] = picked.reshape(plane, ROWS, HD)
        for f in range(0, plane, batch):
            to_group((c, f), q_send, q_recv, 1)
    q_recv[me] = q_send[0]

    sel_t[...] = sel[...].T

    for load in loads[8:10] + loads[12:]:
        load.wait()
    to_smem.wait()
    scale = 1.0 / math.sqrt(HD)
    token = iota((ROWS, block_len), 1)

    def some_lanes(group):
        lanes = lanes_of(group)
        first = group[0] * plane + group[1]
        blocks = [lane_blk[0, d] for d in lanes]
        scored = []
        for j in range(0, batch, 2):
            queries = jnp.concatenate([q_recv[d] for d in lanes[j : j + 2]], axis=0)
            keys = jnp.concatenate([kp[b] for b in blocks[j : j + 2]], axis=0)
            s = lax.dot_general(
                queries, keys, (((1,), (1,)), ((), ())), preferred_element_type=F32
            )
            for h in range(2):
                own = s[h * ROWS : (h + 1) * ROWS, h * block_len : (h + 1) * block_len]
                scored.append(jnp.where(token < fill[blocks[j + h]], own * scale, masked_score))
        s = jnp.concatenate(scored, axis=0)
        peak = jnp.max(s, axis=1, keepdims=True)
        w = jnp.exp(s - peak)
        total = jnp.sum(w, axis=1, keepdims=True)
        w16 = w.astype(BF16)
        mixed = []
        for j in range(0, batch, 2):
            values = jnp.concatenate([vp[b] for b in blocks[j : j + 2]], axis=1)
            m = jnp.dot(w16[j * ROWS : (j + 2) * ROWS], values, preferred_element_type=F32)
            mixed += [m[:ROWS, :HD], m[ROWS:, HD:]]
        mixed = jnp.concatenate(mixed, axis=0)
        tiles = in_spare_row(peak + jnp.log(total), mixed / total).astype(BF16)
        p_send[pl.ds(first, batch)] = tiles

    for lanes_group in groups:
        wait_group(lanes_group, q_recv, 1)
        some_lanes(lanes_group)
        to_group(lanes_group, p_send, p_recv, 2)
        if lanes_group == (1, batch):
            sum_part(1)
    p_recv[me] = p_send[0]

    for load in loads[5:8]:
        load.wait()
    take_part(1)
    low_v = unpacked(low_total[...].astype(F32)[half:])
    up_v = jnp.dot(low_v, vu[...], preferred_element_type=F32)
    value = vb[...].reshape(steps * slots, HD).astype(F32) + adapter_scale * up_v
    value = value.astype(BF16).astype(F32)
    values = [value[t * slots : (t + 1) * slots] for t in range(steps)]
    keys = [kb[t].astype(F32) for t in range(steps)]
    lane_s = iota((slots, HD), 1)
    scores = [jnp.full((slots, HD), masked_score, F32) for _ in range(steps)]
    for r in range(rows):
        q_r = tiles[r].astype(F32)
        for u in range(r // group + 1):
            s = jnp.sum(q_r * keys[u], axis=1, keepdims=True) * scale
            scores[u] = jnp.where(lane_s == r, s, scores[u])
    new_peak = functools.reduce(jnp.maximum, scores)
    new_w = [
        jnp.where(lane_s >= u * group, jnp.exp(scores[u] - new_peak), 0.0) for u in range(steps)
    ]
    new_total = functools.reduce(jnp.add, new_w)
    rounded = [w.astype(BF16).astype(F32) for w in new_w]
    for r in range(rows):
        acc = jnp.zeros((slots, HD), F32)
        for u in range(r // group + 1):
            acc = acc + rounded[u][:, r : r + 1] * values[u]
        new_mixed[pl.ds(r * slots, slots), :] = acc

    def spare_row(c, i):
        d = lane_at(c, i)
        wide[pl.ds(d, 1), :] = p_recv[d].astype(F32)[ROWS - 1 :]

    for c, f in groups:
        wait_group((c, f), p_recv, 2)
        for i in range(f, f + batch):
            spare_row(c, i)
    tags = tagc[...]
    line = wide[...]
    middle, low = pltpu.roll(line, HD - ROWS, 1), pltpu.roll(line, HD - 2 * ROWS, 1)
    lse = jnp.where(tags >= 0.0, line + middle + low, masked_score)
    for s in range(slots):
        mine_s = jnp.where(tags == float(s), lse, masked_score)
        top_s[pl.ds(s, 1), :] = jnp.max(mine_s, axis=0, keepdims=True)
    top = jnp.maximum(top_s[...], new_peak)
    top_s[...] = top
    lane_top = jnp.zeros((peers, HD), F32)
    for s in range(slots):
        lane_top = jnp.where(tags == float(s), top_s[pl.ds(s, 1), :], lane_top)
    weight = jnp.exp(lse - lane_top)
    for s in range(slots):
        mine_s = jnp.where(tags == float(s), weight, 0.0)
        den_s[pl.ds(s, 1), :] = jnp.sum(mine_s, axis=0, keepdims=True)
    new_weight = jnp.exp(new_peak - top)
    inverse = 1.0 / (den_s[...] + new_total * new_weight)
    wide[...] = weight
    on_row = iota((ROWS, HD), 0) == iota((ROWS, HD), 1)

    def weigh(c, i):
        d = lane_at(c, i)
        row = jnp.where(on_row, wide[pl.ds(d, 1), :], 0.0)
        column = jnp.sum(row, axis=1, keepdims=True)
        at = pl.ds((c * plane + i) * ROWS, ROWS)
        weighted[at, :] = (p_recv[d].astype(F32) * column).astype(BF16)

    for c in range(side):
        for i in range(plane):
            weigh(c, i)
    mixed = jnp.dot(sel_t[...], weighted[...], preferred_element_type=F32)
    for r in range(rows):
        t, g = r // group, r % group
        at = slice(r * slots, (r + 1) * slots)
        res = mixed[at] + new_weight[:, r : r + 1] * new_mixed[at, :]
        res = res * inverse[:, r : r + 1]
        out_ref[t, :, g * HD : (g + 1) * HD] = res.astype(BF16)

    @pl.when(is_inner)
    def _():
        for k in range(2):
            wait_for(low_recv.at[0, low_parts[k]], low_send_sem.at[k])
            wait_for(low_recv.at[pl.ds(0, chips - 1), low_parts[k]], low_send_sem.at[k + 2])

    @pl.when(is_outer)
    def _():
        for k in range(2):
            wait_for(low_recv.at[pl.ds(0, n_inner), low_parts[k]], low_send_sem.at[k])

    wait_lanes(tag_recv, send_sem.at[0])
    wait_lanes(q_recv, send_sem.at[1])
    wait_lanes(p_recv, send_sem.at[2])


def on_device(
    x_rows,
    query_base_rows,
    k_base,
    value_base_rows,
    k_pool,
    v_pool,
    block_dest,
    block_slot,
    block_fill,
    a_query,
    query_up_factor,
    a_value,
    value_up_factor,
):
    peers, ranks = lax.axis_size("roll"), lax.axis_size("learn")
    steps, slots, width = x_rows.shape
    pool, block_len, _ = k_pool.shape
    rank = a_query.shape[1]
    a_query, a_value, block_dest = a_query.T, a_value.T, block_dest.T
    group = query_base_rows.shape[2] // HD
    chunk = width // ranks
    dims = (steps, slots, chunk, pool, block_len, group)
    hbm = pl.BlockSpec(memory_space=pltpu.HBM)
    vmem = pltpu.VMEM
    dma = pltpu.SemaphoreType.DMA
    arrays = (
        x_rows,
        query_base_rows,
        k_base,
        value_base_rows,
        k_pool,
        v_pool,
        block_dest,
        block_slot,
        block_fill,
        a_query,
        query_up_factor,
        a_value,
        value_up_factor,
    )
    return pl.pallas_call(
        functools.partial(kernel, peers, ranks, dims),
        out_shape=pltpu.VMEM(query_base_rows.shape, BF16),
        in_specs=[hbm] * 13,
        out_specs=pl.BlockSpec(memory_space=pltpu.VMEM),
        scratch_shapes=[
            vmem((steps, slots, chunk), BF16),
            pltpu.SMEM(block_dest.shape, jnp.int32),
            pltpu.SMEM(block_slot.shape, jnp.int32),
            pltpu.SMEM(block_fill.shape, jnp.int32),
            vmem(query_base_rows.shape, BF16),
            vmem(k_base.shape, BF16),
            vmem(value_base_rows.shape, BF16),
            vmem(k_pool.shape, BF16),
            vmem(v_pool.shape, BF16),
            vmem((2 * rank, chunk), BF16),
            vmem(query_up_factor.shape, BF16),
            vmem(value_up_factor.shape, BF16),
            vmem((1, HD), F32),
            vmem((peers, HD), F32),
            vmem((1, HD), jnp.int32),
            pltpu.SMEM((1, HD), jnp.int32),
            vmem((ranks, steps * slots, 2 * rank), BF16),
            vmem((steps * slots, 2 * rank), BF16),
            vmem((peers, HD), F32),
            vmem((peers * ROWS, ROWS * slots), BF16),
            vmem((ROWS * slots, peers * ROWS), BF16),
            vmem((peers, ROWS, HD), BF16),
            vmem((peers, ROWS, HD), BF16),
            vmem((peers, ROWS, HD), BF16),
            vmem((peers, ROWS, HD), BF16),
            vmem((ROWS * slots, HD), F32),
            vmem((slots, HD), F32),
            vmem((slots, HD), F32),
            vmem((peers, HD), F32),
            vmem((peers * ROWS, HD), BF16),
            dma((13,)),
            dma,
            dma((3,)),
            dma((1,)),
            dma((2, 8)),
            dma((4,)),
            dma((4,)),
            pltpu.SemaphoreType.REGULAR,
            pltpu.SemaphoreType.REGULAR,
        ],
        compiler_params=pltpu.CompilerParams(
            collective_id=0, has_side_effects=True, vmem_limit_bytes=48 * 1024 * 1024
        ),
    )(*[pltpu.with_memory_space_constraint(array, pltpu.HBM) for array in arrays])


def solution(mesh):
    return jax.shard_map(
        on_device,
        mesh=mesh,
        in_specs=(
            P(None, "roll", None),
            P(None, "roll", "learn"),
            P(None, "roll", "learn"),
            P(None, "roll", "learn"),
            P("roll", None, "learn"),
            P("roll", None, "learn"),
            P("roll", None),
            P("roll"),
            P("roll"),
            P("learn", None),
            P(None, "learn"),
            P("learn", None),
            P(None, "learn"),
        ),
        out_specs=P(None, "roll", "learn"),
        check_vma=False,
    )
```
